32 devices in a mesh: lon: 8 (over z, x), ch: 2 (over y), lat: 2 (over core).
Axes of the slice: x: 2, y: 2, z: 4, core: 2. Of those that a mesh axis runs over, the one named last changes fastest.
Arguments:
- features: bfloat16 [40, 256, 2048], P('lat', 'lon', 'ch'), may hold values from -6 to 6
- labels: int32 [40, 256], P('lat', 'lon'), may hold values from 0 to 127
- tile_list: int32 [2, 8, 5], P('lat', 'lon'), may hold values from 0 to 5, as said below
- w_point: bfloat16 [2048, 256], P('ch'), may hold values from -0.125 to 0.125
- w_rates: bfloat16 [3, 9, 2048, 256], P(None, None, 'ch'), may hold values from -0.046875 to 0.046875
- branch_scale: float32 [4, 256], replicated, may hold values from 0.5 to 2
- branch_shift: float32 [4, 256], replicated, may hold values from -3 to 3
- w_proj: bfloat16 [1024, 256], replicated, may hold values from -0.25 to 0.25
- proj_scale: float32 [256], replicated, may hold values from 0.5 to 2
- proj_shift: float32 [256], replicated, may hold values from -3 to 3
- w_class: bfloat16 [256, 128], replicated, may hold values from -1.8 to 1.8
Outputs:
- feature_grad: bfloat16 [40, 256, 2048], P('lat', 'lon', 'ch')
The draws below stay inside these ranges and needn't reach their ends.
Inputs may be any that keep to these rules, and one draw needn't show every extreme that they name: `tile_list`: each entry lists the distinct active tile indices of that block in increasing order, followed by padding entries equal to 5; every block has at least one active tile, some block has all 5, some block exactly one.
All inputs are finite; a program needn't handle non-finite values.
Results may differ from the reference program's by a relative error of at most 0.039.
The reference program's roundings to bfloat16 on the way count: a program that leaves them out, or rounds other values in their place, can miss the bound.
Values may be sent and summed in bfloat16 or wider, within the bound.
No kernel may reach another device: no remote copies, remote signals or barrier semaphores. Data moves between devices by JAX's collectives and lax.ppermute only.
A program may use at most 192 MiB of HBM per device.

```python
import math
import jax
import jax.numpy as jnp

C_IN = 2048
C_OUT = 256
K = 128
H_DEV = 20
W_DEV = 32
TILES_DEV = 5
LAT_BANDS = 2
LON_TILES = 8
H = 40
W = 256


def draw_tile_list(key, part):
    blocks = LAT_BANDS * LON_TILES
    key_count, key_order, key_score = jax.random.split(key, 3)
    counts = jax.random.randint(key_count, (blocks,), 1, TILES_DEV + 1)
    order = jax.random.permutation(key_order, blocks)
    counts = counts.at[order[0]].set(TILES_DEV)
    counts = counts.at[order[1]].set(1)
    tiles = jnp.arange(TILES_DEV, dtype=jnp.int32)
    scores = jax.random.randint(key_score, (blocks, TILES_DEV), 0, 1 << 20) * TILES_DEV + tiles[None, :]
    ranks = jnp.argsort(jnp.argsort(scores, axis=1), axis=1)
    chosen = ranks < counts[:, None]
    keyed = jnp.where(chosen, tiles[None, :], TILES_DEV + tiles[None, :])
    ordered = jnp.sort(keyed, axis=1)
    lists = jnp.where(ordered < TILES_DEV, ordered, TILES_DEV)
    return lists.reshape(LAT_BANDS, LON_TILES, TILES_DEV).astype(jnp.int32)


def draw_w_class(key, part):
    base = jnp.clip(jax.random.normal(key, (C_OUT, K), jnp.float32) * 0.3, -1.8, 1.8)
    return base.astype(jnp.bfloat16)


def touch_ends(result, stream_key, low, high):
    longest = result.shape.index(max(result.shape))
    spots = []
    for shift in (0, 1):
        where = [jax.random.randint(jax.random.fold_in(stream_key, axis), (), 0, length) for axis, length in enumerate(result.shape)]
        where[longest] = (where[longest] + shift) % result.shape[longest]
        spots.append(tuple(where))
    return result.at[spots[0]].set(low).at[spots[1]].set(high)


def steps_of(rng, dims, pieces, least, top_value):
    level, own = 1.0, jax.random.fold_in(rng, 6)
    for axis_at, shards_of in pieces:
        draws = jnp.exp(jax.random.uniform(jax.random.fold_in(own, axis_at), (shards_of,), jnp.float32, least / len(pieces), top_value / len(pieces)))
        level = level * jnp.repeat(draws, dims[axis_at] // shards_of).reshape([-1 if axis == axis_at else 1 for axis in range(len(dims))])
    return level


def scatter_about(stream_key, dims, scale, bound, shards=(), kind=jnp.bfloat16):
    level = steps_of(stream_key, dims, shards, -0.22, 0.18) if shards else 1.0
    entries = jax.random.normal(stream_key, dims, jnp.float32) * scale * level
    return jnp.minimum(jnp.maximum(entries, -bound), bound).astype(kind)


def setup_inputs(seed: int = 0) -> dict:
    streams_of = jax.random.split(jax.random.key(seed), 12)
    return {
        "features": scatter_about(streams_of[0], (H, W, C_IN), 1.0, 6.0, ((0, 2), (1, 8), (2, 2))),
        "labels": touch_ends(jax.random.randint(streams_of[1], (H, W), 0, K), jax.random.fold_in(streams_of[1], 1), 0, K - 1).astype(jnp.int32),
        "tile_list": draw_tile_list(jax.random.fold_in(streams_of[11], 71), 0),
        "w_point": scatter_about(streams_of[3], (C_IN, C_OUT), C_IN ** -0.5, 0.125, ((0, 2),)),
        "w_rates": scatter_about(streams_of[4], (3, 9, C_IN, C_OUT), (9 * C_IN) ** -0.5, 0.046875, ((2, 2),)),
        "branch_scale": jnp.clip(jnp.exp(jax.random.uniform(streams_of[5], (4, C_OUT), jnp.float32, math.log(0.5), math.log(2.0))), 0.5, 2.0),
        "branch_shift": scatter_about(streams_of[6], (4, C_OUT), 0.5, 3.0, (), jnp.float32),
        "w_proj": scatter_about(streams_of[7], (4 * C_OUT, C_OUT), (2 * C_OUT) ** -0.5, 0.25),
        "proj_scale": jnp.clip(jnp.exp(jax.random.uniform(streams_of[8], (C_OUT,), jnp.float32, math.log(0.5), math.log(2.0))), 0.5, 2.0),
        "proj_shift": scatter_about(streams_of[9], (C_OUT,), 0.5, 3.0, (), jnp.float32),
        "w_class": draw_w_class(jax.random.fold_in(streams_of[11], 71), 0),
    }


atrous_rates = (6, 12, 18)


def shift_grid(field, row_off, col_off):
    rolled = jnp.roll(field, -col_off, axis=1)
    if row_off == 0:
        return rolled
    zeros = jnp.zeros((abs(row_off),) + field.shape[1:], field.dtype)
    if row_off > 0:
        return jnp.concatenate([rolled[row_off:], zeros], 0)
    return jnp.concatenate([zeros, rolled[:row_off]], 0)


def reference(features, labels, tile_list, w_point, w_rates, branch_scale, branch_shift, w_proj, proj_scale, proj_shift, w_class):
    height, width = features.shape[0], features.shape[1]
    pixels = height * width
    branches = [jnp.dot(features.reshape(pixels, C_IN), w_point, preferred_element_type=jnp.float32)]
    for branch, rate in enumerate(atrous_rates):
        total = jnp.zeros((pixels, C_OUT), jnp.float32)
        for row_step in (-1, 0, 1):
            for col_step in (-1, 0, 1):
                tap = 3 * (row_step + 1) + (col_step + 1)
                moved = shift_grid(features, row_step * rate, col_step * rate).reshape(pixels, C_IN)
                total = total + jnp.dot(moved, w_rates[branch, tap], preferred_element_type=jnp.float32)
        branches.append(total)
    pre_all = [branches[b] * branch_scale[b] + branch_shift[b] for b in range(4)]
    joined = jnp.concatenate([jax.nn.relu(p) for p in pre_all], 1).astype(jnp.bfloat16)
    z_pre = jnp.dot(joined, w_proj, preferred_element_type=jnp.float32) * proj_scale + proj_shift
    hidden = jax.nn.relu(z_pre).astype(jnp.bfloat16)
    logits = jnp.dot(hidden, w_class, preferred_element_type=jnp.float32)
    shifted = logits - jnp.max(logits, axis=1, keepdims=True)
    expo = jnp.exp(shifted)
    prob = expo / jnp.sum(expo, axis=1, keepdims=True)
    onehot = (labels.reshape(pixels)[:, None] == jnp.arange(K, dtype=jnp.int32)[None, :]).astype(jnp.float32)
    rows_i = jnp.arange(height, dtype=jnp.int32)
    cols_j = jnp.arange(width, dtype=jnp.int32)
    local_tile = ((rows_i[:, None] % H_DEV) * W_DEV + cols_j[None, :] % W_DEV) // 128
    lists_full = jnp.repeat(jnp.repeat(tile_list, H_DEV, axis=0), W_DEV, axis=1)
    active = jnp.any(lists_full == local_tile[:, :, None], axis=2).astype(jnp.float32).reshape(pixels)
    d_logits = (active[:, None] * (prob - onehot)).astype(jnp.bfloat16)
    d_hidden = jnp.dot(d_logits, w_class.T, preferred_element_type=jnp.float32)
    d_z = (d_hidden * proj_scale * (z_pre > 0).astype(jnp.float32)).astype(jnp.bfloat16)
    d_joined = jnp.dot(d_z, w_proj.T, preferred_element_type=jnp.float32)
    d_branches = [(d_joined[:, b * C_OUT:(b + 1) * C_OUT] * branch_scale[b] * (pre_all[b] > 0).astype(jnp.float32)).astype(jnp.bfloat16) for b in range(4)]
    grad = jnp.dot(d_branches[0], w_point.T, preferred_element_type=jnp.float32)
    for branch, rate in enumerate(atrous_rates):
        grad_map = d_branches[branch + 1].reshape(height, width, C_OUT)
        for row_step in (-1, 0, 1):
            for col_step in (-1, 0, 1):
                tap = 3 * (row_step + 1) + (col_step + 1)
                moved = shift_grid(grad_map, -row_step * rate, -col_step * rate).reshape(pixels, C_OUT)
                grad = grad + jnp.dot(moved, w_rates[branch, tap].T, preferred_element_type=jnp.float32)
    return grad.reshape(height, width, C_IN).astype(jnp.bfloat16)
```

```python
import functools

import jax
import jax.numpy as jnp
from jax import lax
from jax.experimental import pallas as pl
from jax.experimental.pallas import tpu as pltpu
from jax.sharding import PartitionSpec as P

atrous_rates = (6, 12, 18)
halo_at = (30, 18, 0)
halo_cols = 36
f32 = jnp.float32
bf16 = jnp.bfloat16
wire = jnp.float16
vmem_bytes = 44 * 1024 * 1024


def mul(lhs, rhs):
    return jnp.dot(lhs, rhs, preferred_element_type=f32)


def mul_t(lhs, rhs):
    return lax.dot_general(lhs, rhs, (((1,), (1,)), ((), ())), preferred_element_type=f32)


def call(body, grid, in_specs, out_specs, out_shape, scratch, flops, moved):
    return pl.pallas_call(
        body,
        grid_spec=pltpu.PrefetchScalarGridSpec(
            num_scalar_prefetch=1,
            grid=grid,
            in_specs=in_specs,
            out_specs=out_specs,
            scratch_shapes=scratch,
        ),
        out_shape=out_shape,
        compiler_params=pltpu.CompilerParams(
            vmem_limit_bytes=vmem_bytes, dimension_semantics=("arbitrary",) * len(grid)
        ),
        cost_estimate=pl.CostEstimate(flops=flops, bytes_accessed=moved, transcendentals=0),
    )


def whole(shape):
    return pl.BlockSpec(shape, lambda *_: (0,) * len(shape))


def side_own(rows, cols):
    def body(place, feat, weight, out):
        pixels = rows * cols
        out[0, 0] = mul(feat[...], weight[0, 1, 0])
        for branch, rate in enumerate(atrous_rates):
            cut = rate * cols

            @pl.when(pl.program_id(0) == 2 - branch)
            def _():
                out[0, 0, cut:, :] += mul(feat[: pixels - cut, :], weight[0, 0, 0])
                out[0, 0, : pixels - cut, :] += mul(feat[cut:, :], weight[0, 2, 0])

    return body


def side_other(rows, cols, halves):
    part = rows // halves

    def body(place, acc, other, weight, local_sum, halo, total):
        lat, ch = place[0], place[1]
        step = pl.program_id(1)
        for branch, rate in enumerate(atrous_rates):
            at = halo_at[branch]

            @pl.when(pl.program_id(0) == 2 - branch)
            def _():
                source = pl.multiple_of(lat * ((rows - rate) * cols), cols)
                extra = mul(other[pl.ds(source, rate * cols), :], weight[0, 0, 0])
                total[...] = acc[0, 0].reshape(total.shape)
                total[pl.ds((1 - lat) * (rows - rate), rate)] += extra.reshape(
                    rate, cols, extra.shape[1]
                )

                @pl.when(step == 0)
                def _():
                    local_sum[0, :, rate:, :] = total[:, : cols - rate, :]
                    local_sum[0, :, :rate, :] = jnp.zeros_like(total[:, :rate, :])
                    for half in range(halves):
                        slot = 0 if halves == 1 else (ch if half else 1 - ch)
                        halo[slot, 1, :, at : at + rate, :] = total[
                            half * part : (half + 1) * part, cols - rate :, :
                        ]

                @pl.when(step == 1)
                def _():
                    local_sum[0, :, : cols - rate, :] += total[:, rate:, :]
                    for half in range(halves):
                        slot = 0 if halves == 1 else (ch if half else 1 - ch)
                        halo[slot, 0, :, at : at + rate, :] = total[
                            half * part : (half + 1) * part, :rate, :
                        ]

    return body


def centre(rows, cols, halves):
    pixels = rows * cols
    part = pixels // halves

    def body(place, feat, other, point, weight, local_sum, out, total):
        lat, ch = place[0], place[1]
        step = pl.program_id(0)

        @pl.when(step == 0)
        def _():
            total[...] = mul(feat[...], point[...])

        @pl.when(step > 0)
        def _():
            total[...] = mul(feat[...], weight[0, 1, 0]) + local_sum[0].reshape(total.shape)

        for branch, rate in enumerate(atrous_rates):
            cut = rate * cols

            @pl.when(step == branch + 1)
            def _():
                total[cut:, :] += mul(feat[: pixels - cut, :], weight[0, 0, 0])
                total[: pixels - cut, :] += mul(feat[cut:, :], weight[0, 2, 0])
                source = pl.multiple_of(lat * (pixels - cut), cols)
                target = pl.multiple_of((1 - lat) * (pixels - cut), cols)
                total[pl.ds(target, cut), :] += mul(
                    other[pl.ds(source, cut), :], weight[0, 2 * (1 - lat), 0]
                )

        for half in range(halves):
            slot = 0 if halves == 1 else (ch if half else 1 - ch)
            out[slot] = total[half * part : (half + 1) * part, :]

    return body


def head(rows, cols, width):
    pixels = rows * cols

    def body(
        place, own, came, from_left, from_right, labels, active, scale, shift,
        w_proj, proj_scale, proj_shift, w_class, out, to_left, to_right, total, grad,
    ):
        total[...] = (own[...] + came[...]).reshape(total.shape)
        for branch, rate in enumerate(atrous_rates):
            at, lanes = halo_at[branch], slice((branch + 1) * width, (branch + 2) * width)
            total[:, :rate, lanes] += from_left[:, at : at + rate, :].astype(f32)
            total[:, cols - rate :, lanes] += from_right[:, at : at + rate, :].astype(f32)
        pre = total[...].reshape(pixels, 4 * width) * scale[...] + shift[...]
        joined = jnp.maximum(pre, 0.0).astype(bf16)
        z_pre = mul(joined, w_proj[...]) * proj_scale[...] + proj_shift[...]
        hidden = jnp.maximum(z_pre, 0.0).astype(bf16)
        logits = mul(hidden, w_class[...])
        expo = jnp.exp(logits - jnp.max(logits, axis=1, keepdims=True))
        prob = expo / jnp.sum(expo, axis=1, keepdims=True)
        ids = lax.broadcasted_iota(jnp.int32, prob.shape, 1)
        onehot = jnp.where(ids == labels[...], 1.0, 0.0)
        d_logits = (active[...] * (prob - onehot)).astype(bf16)
        d_hidden = mul_t(d_logits, w_class[...]) * proj_scale[...]
        d_z = jnp.where(z_pre > 0, d_hidden, 0.0).astype(bf16)
        d_joined = mul_t(d_z, w_proj[...]) * scale[...]
        d_all = jnp.where(pre > 0, d_joined, 0.0)
        grad[...] = d_all.reshape(grad.shape)
        out[...] = grad[...].astype(bf16)
        for branch, rate in enumerate(atrous_rates):
            at, lanes = halo_at[branch], slice((branch + 1) * width, (branch + 2) * width)
            to_left[:, at : at + rate, :] = grad[:, :rate, lanes].astype(bf16)
            to_right[:, at : at + rate, :] = grad[:, cols - rate :, lanes].astype(bf16)

    return body


def back_local(rows, cols, width, halves):
    pixels = rows * cols
    part = rows // halves

    def body(place, *refs):
        mine, others = refs[:halves], refs[halves : 2 * halves]
        point, weight, out, maps, other_maps = refs[2 * halves :]
        lat, ch = place[0], place[1]
        step = pl.program_id(0)

        @pl.when(step == 0)
        def _():
            for index in range(halves):
                first = 0 if halves == 1 else (1 - ch if index else ch) * part
                at_rows = pl.ds(first, part)
                spot = pl.ds(pl.multiple_of(first * cols, cols), part * cols)
                block = mine[index][:, :, :width].reshape(part * cols, width)
                out[spot, :] = mul_t(block, point[...])
                for branch, rate in enumerate(atrous_rates):
                    lanes = slice((branch + 1) * width, (branch + 2) * width)
                    over = slice(branch * width, (branch + 1) * width)
                    for value, kept in (
                        (mine[index][:, :, lanes].astype(f32), maps),
                        (others[index][:, :, over].astype(f32), other_maps),
                    ):
                        zeros = jnp.zeros_like(value[:, :rate, :])
                        left = jnp.concatenate([value[:, rate:, :], zeros], 1)
                        right = jnp.concatenate([zeros, value[:, : cols - rate, :]], 1)
                        kept[3 * branch, at_rows] = left.astype(bf16)
                        kept[3 * branch + 1, at_rows] = value.astype(bf16)
                        kept[3 * branch + 2, at_rows] = right.astype(bf16)

        for branch, rate in enumerate(atrous_rates):
            cut = rate * cols

            @pl.when((step > 3 * branch) & (step <= 3 * branch + 3))
            def _():
                field = maps[step - 1].reshape(pixels, width)
                out[...] += mul_t(field, weight[0, 1, 0])
                out[cut:, :] += mul_t(field[: pixels - cut, :], weight[0, 2, 0])
                out[: pixels - cut, :] += mul_t(field[cut:, :], weight[0, 0, 0])
                target = pl.multiple_of((1 - lat) * (pixels - cut), cols)
                taken = other_maps[step - 1, pl.ds(lat * (rows - rate), rate)]
                out[pl.ds(target, cut), :] += mul_t(
                    taken.reshape(cut, width), weight[0, 2 * lat, 0]
                )

    return body


def back_halo(rows, cols, width, halves):
    part = rows // halves

    def body(place, *refs):
        mine, others = refs[:halves], refs[halves : 2 * halves]
        acc, weight, out, total, maps, other_maps = refs[2 * halves :]
        lat, ch = place[0], place[1]
        step = pl.program_id(0)

        @pl.when(step == 0)
        def _():
            total[...] = acc[...].reshape(total.shape)

        for branch, rate in enumerate(atrous_rates):
            at, window = halo_at[branch], -(-rate // 8) * 8
            for side in range(2):

                @pl.when(step == 2 * (2 - branch) + side)
                def _():
                    for index in range(halves):
                        first = 0 if halves == 1 else (1 - ch if index else ch) * part
                        for source, kept in ((mine[index], maps), (others[index], other_maps)):
                            value = source[side, :, at : at + rate, :].astype(f32)
                            if window > rate:
                                blank = jnp.zeros((part, window - rate, width), f32)
                                both = [value, blank] if side == 0 else [blank, value]
                                value = jnp.concatenate(both, 1)
                            kept[pl.ds(first, part), :window, :] = value
                    place_cols = slice(0, window) if side == 0 else slice(cols - window, cols)

                    def add(to_first, from_first, count, tap, store):
                        field = store[pl.ds(from_first, count), :window, :].astype(bf16)
                        product = mul_t(field.reshape(count * window, width), tap)
                        total[pl.ds(to_first, count), place_cols, :] += product.reshape(
                            count, window, product.shape[1]
                        )

                    add(0, 0, rows, weight[0, 1, 0], maps)
                    add(rate, 0, rows - rate, weight[0, 2, 0], maps)
                    add(0, rate, rows - rate, weight[0, 0, 0], maps)
                    edge = rows - rate
                    add((1 - lat) * edge, lat * edge, rate, weight[0, 2 * lat, 0], other_maps)

        @pl.when(step == 5)
        def _():
            out[...] = total[...].astype(bf16)

    return body


def shift_pairs(size, step):
    return [(i, (i + step) % size) for i in range(size)]


def local(
    features, labels, tile_list, w_point, w_rates, branch_scale, branch_shift,
    w_proj, proj_scale, proj_shift, w_class,
):
    rows, cols, chans = features.shape
    pixels = rows * cols
    width = w_point.shape[1]
    ids = w_class.shape[1]
    lon_size, ch_size, lat_size = (lax.axis_size(a) for a in ("lon", "ch", "lat"))
    assert lat_size == 2 and max(atrous_rates) <= min(rows, cols)
    halves = 2 if ch_size == 2 else 1
    part = rows // halves
    lat, ch = lax.axis_index("lat"), lax.axis_index("ch")
    place = jnp.stack([lat, ch]).astype(jnp.int32)
    taps = w_rates.reshape(3, 3, 3, chans, width)
    tap_flops = 2 * pixels * chans * width
    tap_bytes = 2 * chans * width

    def swap_lat(value):
        return lax.ppermute(value, "lat", shift_pairs(2, 1))

    def swap_ch(value):
        return lax.ppermute(value, "ch", shift_pairs(2, 1))

    def to_left(value):
        return lax.ppermute(value, "lon", shift_pairs(lon_size, -1))

    def to_right(value):
        return lax.ppermute(value, "lon", shift_pairs(lon_size, 1))

    feat = features.reshape(pixels, chans)
    other = swap_lat(feat)

    sides = call(
        side_own(rows, cols),
        (3, 2),
        [
            whole((pixels, chans)),
            pl.BlockSpec((1, 3, 1, chans, width), lambda k, v, _: (2 - k, 0, 2 * v, 0, 0)),
        ],
        pl.BlockSpec((1, 1, pixels, width), lambda k, v, _: (k, v, 0, 0)),
        jax.ShapeDtypeStruct((3, 2, pixels, width), f32),
        [],
        11 * tap_flops,
        18 * tap_bytes,
    )(place, feat, taps)
    halo_shape = (halves, 2, part, halo_cols, width)
    local_sum, halo = call(
        side_other(rows, cols, halves),
        (3, 2),
        [
            pl.BlockSpec((1, 1, pixels, width), lambda k, v, _: (k, v, 0, 0)),
            whole((pixels, chans)),
            pl.BlockSpec(
                (1, 1, 1, chans, width), lambda k, v, s: (2 - k, 2 * (1 - s[0]), 2 * v, 0, 0)
            ),
        ],
        [
            pl.BlockSpec((1, rows, cols, width), lambda k, v, _: (2 - k, 0, 0, 0)),
            whole(halo_shape),
        ],
        [
            jax.ShapeDtypeStruct((3, rows, cols, width), f32),
            jax.ShapeDtypeStruct(halo_shape, f32),
        ],
        [pltpu.VMEM((rows, cols, width), f32)],
        4 * tap_flops,
        6 * tap_bytes,
    )(place, sides, other, taps)

    main = call(
        centre(rows, cols, halves),
        (4,),
        [
            whole((pixels, chans)),
            whole((pixels, chans)),
            whole((chans, width)),
            pl.BlockSpec(
                (1, 3, 1, chans, width), lambda b, _: (jnp.maximum(b - 1, 0), 0, 1, 0, 0)
            ),
            pl.BlockSpec(
                (1, rows, cols, width), lambda b, _: (jnp.maximum(b - 1, 0), 0, 0, 0)
            ),
        ],
        pl.BlockSpec((halves, pixels // halves, width), lambda b, _: (0, 0, b)),
        jax.ShapeDtypeStruct((halves, pixels // halves, 4 * width), f32),
        [pltpu.VMEM((pixels, width), f32)],
        10 * tap_flops,
        10 * tap_bytes,
    )(place, feat, other, w_point, taps, local_sum)

    if halves == 2:
        halo_sum = halo[1] + swap_ch(halo[0].astype(wire)).astype(f32)
        own, came = main[1], swap_ch(main[0].astype(wire)).astype(f32)
    else:
        halo_sum = lax.psum(halo[0], "ch")
        own = lax.psum(main[0], "ch")
        came = jnp.zeros_like(own)
    from_right = to_left(halo_sum[0].astype(wire)).astype(f32)
    from_left = to_right(halo_sum[1].astype(wire)).astype(f32)

    pixel = jnp.arange(pixels, dtype=jnp.int32)
    active = jnp.any(tile_list.reshape(1, -1) == (pixel // 128)[:, None], axis=1).astype(f32)
    count = pixels // halves
    first = ch * count if halves == 2 else 0
    label_part = lax.dynamic_slice(labels.reshape(pixels, 1), (first, 0), (count, 1))
    active_part = lax.dynamic_slice(active.reshape(pixels, 1), (first, 0), (count, 1))

    halo_part = (part, halo_cols, width)
    head_shapes = (
        (count, 4 * width), (count, 4 * width), halo_part, halo_part, (count, 1), (count, 1),
        (1, 4 * width), (1, 4 * width), (4 * width, width), (1, width), (1, width), (width, ids),
    )
    d_mine, edge_left, edge_right = call(
        head(part, cols, width),
        (1,),
        [whole(s) for s in head_shapes],
        [whole((part, cols, 4 * width)), whole(halo_part), whole(halo_part)],
        [
            jax.ShapeDtypeStruct((part, cols, 4 * width), bf16),
            jax.ShapeDtypeStruct(halo_part, bf16),
            jax.ShapeDtypeStruct(halo_part, bf16),
        ],
        [pltpu.VMEM((part, cols, 4 * width), f32), pltpu.VMEM((part, cols, 4 * width), f32)],
        2 * count * width * (8 * width + 2 * ids),
        8 * count * width * 4,
    )(
        place, own, came, from_left, from_right, label_part, active_part,
        branch_scale.reshape(1, -1), branch_shift.reshape(1, -1), w_proj,
        proj_scale.reshape(1, -1), proj_shift.reshape(1, -1), w_class,
    )

    halo_mine = jnp.stack([to_right(edge_right), to_left(edge_left)])
    d_parts, halo_parts = [d_mine], [halo_mine]
    if halves == 2:
        d_parts.append(swap_ch(d_mine))
        halo_parts.append(swap_ch(halo_mine))
    d_others = [swap_lat(d[:, :, width:]) for d in d_parts]
    halo_others = [swap_lat(h) for h in halo_parts]

    grad = call(
        back_local(rows, cols, width, halves),
        (10,),
        [whole((part, cols, 4 * width))] * halves
        + [whole((part, cols, 3 * width))] * halves
        + [
            whole((chans, width)),
            pl.BlockSpec(
                (1, 3, 1, chans, width),
                lambda s, _: (jnp.maximum(s - 1, 0) // 3, 0, jnp.maximum(s - 1, 0) % 3, 0, 0),
            ),
        ],
        whole((pixels, chans)),
        jax.ShapeDtypeStruct((pixels, chans), f32),
        [pltpu.VMEM((9, rows, cols, width), bf16), pltpu.VMEM((9, rows, cols, width), bf16)],
        28 * tap_flops,
        28 * tap_bytes,
    )(place, *d_parts, *d_others, w_point, taps)

    return call(
        back_halo(rows, cols, width, halves),
        (6,),
        [whole((2,) + halo_part)] * (2 * halves)
        + [
            whole((pixels, chans)),
            pl.BlockSpec(
                (1, 3, 1, chans, width), lambda s, _: (2 - s // 2, 0, 2 - 2 * (s % 2), 0, 0)
            ),
        ],
        whole((rows, cols, chans)),
        jax.ShapeDtypeStruct((rows, cols, chans), bf16),
        [
            pltpu.VMEM((rows, cols, chans), f32),
            pltpu.VMEM((rows, 24, width), f32),
            pltpu.VMEM((rows, 24, width), f32),
        ],
        9 * tap_flops,
        18 * tap_bytes,
    )(place, *halo_parts, *halo_others, grad, taps)


def solution(mesh):
    placed = (
        P("lat", "lon", "ch"),
        P("lat", "lon"),
        P("lat", "lon", None),
        P("ch", None),
        P(None, None, "ch", None),
        P(),
        P(),
        P(),
        P(),
        P(),
        P(),
    )
    return jax.shard_map(
        local, mesh=mesh, in_specs=placed, out_specs=P("lat", "lon", "ch"), check_vma=False
    )
```

```python
import functools

import jax
import jax.numpy as jnp
from jax import lax
from jax.experimental import pallas as pl
from jax.experimental.pallas import tpu as pltpu
from jax.sharding import PartitionSpec as P

atrous_rates = (6, 12, 18)
f32 = jnp.float32
bf16 = jnp.bfloat16
wire = jnp.float16
mebi = 1024 * 1024
groups = (((2, 0), (0, 18), 24), ((1,), (0,), 12))
halo_at = (30, 18, 0)
halo_cols = 36


def mul(lhs, rhs):
    return jnp.dot(lhs, rhs, preferred_element_type=f32)


def mul_t(lhs, rhs):
    return lax.dot_general(lhs, rhs, (((1,), (1,)), ((), ())), preferred_element_type=f32)


def call(body, kinds, out_shape, scratch, flops, moved, vmem=16):
    space = {"s": pltpu.SMEM, "v": pltpu.VMEM, "h": pltpu.HBM}
    return pl.pallas_call(
        body,
        in_specs=[pl.BlockSpec(memory_space=space[k]) for k in kinds],
        out_specs=jax.tree.map(lambda _: pl.BlockSpec(memory_space=pltpu.VMEM), out_shape),
        out_shape=out_shape,
        scratch_shapes=scratch,
        compiler_params=pltpu.CompilerParams(vmem_limit_bytes=vmem * mebi),
        cost_estimate=pl.CostEstimate(
            flops=flops // 16, bytes_accessed=moved // 16, transcendentals=0
        ),
    )


def shape(dims, kind):
    return jax.ShapeDtypeStruct(dims, kind)


def slot_of(half, halves, ch):
    return 0 if halves == 1 else (ch if half else 1 - ch)


def beside(*values):
    return values[0] if len(values) == 1 else jnp.concatenate(values, 1)


def point_kernel(halves):
    def body(place, feat, point, out, field, held, arrived):
        count = out.shape[1]
        copies = [
            pltpu.make_async_copy(feat, field, arrived.at[0]),
            pltpu.make_async_copy(point, held, arrived.at[1]),
        ]
        for copy in copies:
            copy.start()
        for copy in copies:
            copy.wait()
        total = mul(field[...], held[...])
        for half in range(halves):
            out[slot_of(half, halves, place[1])] = total[half * count : (half + 1) * count, :]

    return body


def column_steps(total, tall, taps, branch, cols_of, rows, cols):
    pixels, cut = rows * cols, atrous_rates[branch] * cols

    def row_step(u):
        start = pixels + (u - 1) * cut
        return mul(tall[start : start + pixels, :], beside(*(taps(branch, u, v) for v in cols_of)))

    total[...] = (row_step(0) + row_step(1) + row_step(2)).reshape(total.shape)


def side_taps(branches):
    return [(b, u, v) for b in branches for u in range(3) for v in (0, 2)]


def centre_taps(branches):
    return [(b, u, 1) for b in branches for u in range(3)]


def fetcher(taps, held, arrived, wanted):
    copies = [
        pltpu.make_async_copy(taps.at[tap], held.at[i], arrived.at[i])
        for i, tap in enumerate(wanted)
    ]
    for copy in copies:
        copy.start()

    def ready(branch):
        for copy, tap in zip(copies, wanted):
            if tap[0] == branch:
                copy.wait()

    return ready, lambda *tap: held[wanted.index(tap)]


def side_kernel(rows, cols, halves, branches, spots, builds):
    part, pixels = rows // halves, rows * cols
    wanted = side_taps(branches)

    def body(place, *refs):
        if builds:
            feat, other, all_taps, local_sum, halo, tall, total, held, arrived, now = refs
        else:
            tall, all_taps, local_sum, halo, total, held, arrived = refs
        lat, ch = place[0], place[1]
        width = total.shape[-1] // 2
        if builds:
            mine = pltpu.make_async_copy(feat, tall.at[pl.ds(pixels, pixels)], now)
            mine.start()
        ready, taps = fetcher(all_taps, held, arrived, wanted)
        if builds:
            spot = pl.multiple_of((1 - lat) * (2 * pixels), pixels)
            blank = pl.multiple_of(lat * (2 * pixels), pixels)
            tall[pl.ds(spot, pixels), :] = other[...]
            tall[pl.ds(blank, pixels), :] = jnp.zeros((pixels, tall.shape[1]), bf16)
            mine.wait()
        for index, (branch, at) in enumerate(zip(branches, spots)):
            rate = atrous_rates[branch]
            ready(branch)
            column_steps(total, tall, taps, branch, (0, 2), rows, cols)
            for half in range(halves):
                slot, its = slot_of(half, halves, ch), slice(half * part, (half + 1) * part)
                halo[slot, 1, :, at : at + rate, :] = total[its, cols - rate :, :width]
                halo[slot, 0, :, at : at + rate, :] = total[its, :rate, width:]
            local_sum[index, :, rate:, :] = total[:, : cols - rate, :width]
            local_sum[index, :, :rate, :] = jnp.zeros((rows, rate, width), f32)
            local_sum[index, :, : cols - rate, :] += total[:, rate:, width:]

    return body


def centre_kernel(rows, cols, halves):
    part = rows // halves

    def body(place, tall, all_taps, *refs):
        local_sums, (out, total, held, arrived) = refs[: len(groups)], refs[len(groups) :]
        order = [b for g in groups for b in g[0]]
        ready, taps = fetcher(all_taps, held, arrived, centre_taps(order))
        width = total.shape[-1]
        for number, (branches, _, _) in enumerate(groups):
            for index, branch in enumerate(branches):
                ready(branch)
                column_steps(total, tall, taps, branch, (1,), rows, cols)
                for half in range(halves):
                    its = slice(half * part, (half + 1) * part)
                    value = total[its] + local_sums[number][index, its]
                    slot = slot_of(half, halves, place[1])
                    out[slot, :, branch * width : (branch + 1) * width] = value.reshape(
                        part * cols, width
                    )

    return body


def head_kernel(rows, cols, width):
    pixels = rows * cols

    def body(
        place, own_point, came_point, own, came, left_a, right_a, left_b, right_b,
        labels, active, scale, shift, w_proj, proj_scale, proj_shift, w_class,
        d_point, d_side, to_left, to_right, total, grad,
    ):
        total[:, :, :width] = (own_point[...] + came_point[...]).reshape(rows, cols, width)
        total[:, :, width:] = (own[...] + came[...]).reshape(rows, cols, 3 * width)
        edges = ((left_a, right_a), (left_b, right_b))
        for (branches, spots, _), (left, right) in zip(groups, edges):
            for branch, at in zip(branches, spots):
                rate = atrous_rates[branch]
                lanes = slice((branch + 1) * width, (branch + 2) * width)
                total[:, :rate, lanes] += left[:, at : at + rate, :]
                total[:, cols - rate :, lanes] += right[:, at : at + rate, :]
        pre = total[...].reshape(pixels, 4 * width) * scale[...] + shift[...]
        joined = jnp.maximum(pre, 0.0).astype(bf16)
        z_pre = mul(joined, w_proj[...]) * proj_scale[...] + proj_shift[...]
        hidden = jnp.maximum(z_pre, 0.0).astype(bf16)
        logits = mul(hidden, w_class[...])
        expo = jnp.exp(logits - jnp.max(logits, axis=1, keepdims=True))
        prob = expo / jnp.sum(expo, axis=1, keepdims=True)
        ids = lax.broadcasted_iota(jnp.int32, prob.shape, 1)
        onehot = jnp.where(ids == labels[...], 1.0, 0.0)
        d_logits = (active[...] * (prob - onehot)).astype(bf16)
        d_hidden = mul_t(d_logits, w_class[...]) * proj_scale[...]
        d_z = jnp.where(z_pre > 0, d_hidden, 0.0).astype(bf16)
        d_joined = mul_t(d_z, w_proj[...]) * scale[...]
        grad[...] = jnp.where(pre > 0, d_joined, 0.0).reshape(grad.shape)
        d_point[...] = grad[:, :, :width].astype(bf16)
        d_side[...] = grad[:, :, width:].astype(bf16)
        for branch, rate in enumerate(atrous_rates):
            at, lanes = halo_at[branch], slice((branch + 1) * width, (branch + 2) * width)
            to_left[:, at : at + rate, :] = grad[:, :rate, lanes].astype(bf16)
            to_right[:, at : at + rate, :] = grad[:, cols - rate :, lanes].astype(bf16)

    return body


def spread(total, field, taps, branch, steps, begin, same_band, lat, rows, part, cols):
    rate = atrous_rates[branch]

    def add(source, target, count, u):
        weights = beside(*(taps[branch, u, v] for v in steps))
        lhs = field[pl.ds(pl.multiple_of(source * cols, cols), count * cols), :]
        product = mul_t(lhs[:, : len(steps) * weights.shape[1] // len(steps)], weights)
        total[pl.ds(target, count)] += product.reshape(count, cols, product.shape[1])

    if same_band:
        first = begin == 0
        add(0, begin, part, 1)
        inward = min(part, rows - rate)
        add(
            jnp.where(first, 0, part - inward),
            jnp.where(first, rate, rows - inward - rate),
            inward,
            jnp.where(first, 2, 0),
        )
        if part > rate:
            outward = part - rate
            add(
                jnp.where(first, rate, 0),
                jnp.where(first, 0, rows - outward),
                outward,
                jnp.where(first, 0, 2),
            )
    else:
        u = 2 * lat
        near, far = min(rate, part), rate - part
        is_near = (begin == 0) == (lat == 0) if part < rows else True

        def near_rows():
            add(lat * (part - near), (1 - lat) * (rows - rate) + lat * (rate - near), near, u)

        if part == rows:
            near_rows()
        else:
            pl.when(is_near)(near_rows)
            if far > 0:

                @pl.when(jnp.logical_not(is_near))
                def _():
                    add(lat * (part - far), (1 - lat) * (rows - rate + part), far, u)


back_order = (2, 1, 0)


def back_local_kernel(rows, cols, width, halves, mine, first):
    part = rows // halves

    def body(place, own, other, all_taps, *refs):
        total, fields, taps, arrived = refs[-4:]
        copies = [
            pltpu.make_async_copy(all_taps.at[b], taps.at[b], arrived.at[b]) for b in back_order
        ]
        for copy in copies:
            copy.start()
        lat, ch = place[0], place[1]
        begin = 0 if halves == 1 else (ch if mine else 1 - ch) * part
        total[...] = jnp.zeros_like(total) if first else refs[0][...]
        for copy, branch in zip(copies, back_order):
            rate = atrous_rates[branch]
            lanes = slice(branch * width, (branch + 1) * width)
            for source, same_band in ((own, True), (other, False)):
                field = fields.at[2 * branch + same_band]
                value = source[:, :, lanes].astype(f32)
                zeros = jnp.zeros((part, rate, width), f32)
                left = jnp.concatenate([value[:, rate:, :], zeros], 1)
                right = jnp.concatenate([zeros, value[:, : cols - rate, :]], 1)
                for step, shifted in enumerate((left, value, right)):
                    field[:, step * width : (step + 1) * width] = shifted.reshape(
                        part * cols, width
                    ).astype(bf16)
                if same_band:
                    copy.wait()
                spread(
                    total, field, taps, branch, (0, 1, 2), begin, same_band, lat, rows, part, cols
                )

    return body


def back_halo_kernel(rows, cols, width, halves, mine, last):
    part = rows // halves

    def body(place, own, other, point, all_taps, acc, out, fields, taps, arrived, *refs):
        copies = {
            (b, u, v): pltpu.make_async_copy(
                all_taps.at[b, u, v], taps.at[b, u, v], arrived.at[b, u, v]
            )
            for b in back_order
            for u in range(3)
            for v in (0, 2)
        }
        for copy in copies.values():
            copy.start()
        total = refs[0] if last else out
        total[...] = acc[...]
        lat, ch = place[0], place[1]
        begin = 0 if halves == 1 else (ch if mine else 1 - ch) * part
        block = own[:, 2 * halo_cols :, :].reshape(part * cols, width)
        product = mul_t(block, point[...])
        total[pl.ds(begin, part)] += product.reshape(part, cols, product.shape[1])
        for branch in back_order:
            rate, at = atrous_rates[branch], halo_at[branch]
            for source, same_band in ((own, True), (other, False)):
                field = fields.at[2 * branch + same_band]
                left = source[:, at : at + rate, :].astype(f32)
                right = source[:, halo_cols + at : halo_cols + at + rate, :].astype(f32)
                zeros = jnp.zeros((part, cols - rate, width), f32)
                for step, value in enumerate(
                    (jnp.concatenate([left, zeros], 1), jnp.concatenate([zeros, right], 1))
                ):
                    field[:, step * width : (step + 1) * width] = value.reshape(
                        part * cols, width
                    ).astype(bf16)
                if same_band:
                    for tap, copy in copies.items():
                        if tap[0] == branch:
                            copy.wait()
                spread(total, field, taps, branch, (2, 0), begin, same_band, lat, rows, part, cols)
        if last:
            out[...] = total[...].astype(bf16)

    return body


def shift_pairs(size, step):
    return [(i, (i + step) % size) for i in range(size)]


def after(value, *first):
    return lax.optimization_barrier((value, *first))[0]


def local(
    features, labels, tile_list, w_point, w_rates, branch_scale, branch_shift,
    w_proj, proj_scale, proj_shift, w_class,
):
    rows, cols, chans = features.shape
    pixels = rows * cols
    width = w_point.shape[1]
    lon_size, ch_size, lat_size = (lax.axis_size(a) for a in ("lon", "ch", "lat"))
    assert lat_size == 2 and max(atrous_rates) <= min(rows, cols)
    halves = 2 if ch_size == 2 else 1
    part = rows // halves
    count = pixels // halves
    lat, ch = lax.axis_index("lat"), lax.axis_index("ch")
    place = jnp.stack([lat, ch]).astype(jnp.int32)
    taps = w_rates.reshape(3, 3, 3, chans, width)
    tap_flops = 2 * pixels * chans * width
    tap_bytes = 2 * chans * width

    def swap_lat(value):
        return lax.ppermute(value, "lat", shift_pairs(2, 1))

    def swap_ch(value):
        return lax.ppermute(value, "ch", shift_pairs(2, 1))

    def to_left(value):
        return lax.ppermute(value, "lon", shift_pairs(lon_size, -1))

    def to_right(value):
        return lax.ppermute(value, "lon", shift_pairs(lon_size, 1))

    gone = []

    def reduce_ch(parts):
        if halves == 2:
            sent = parts[0].astype(wire)
            gone.append(sent)
            return parts[1], swap_ch(sent)
        own = lax.psum(parts[0], "ch")
        return own, jnp.zeros(own.shape, wire)

    feat = features.reshape(pixels, chans)
    other = swap_lat(feat)
    tall_shape = shape((3 * pixels, chans), bf16)

    main = call(
        point_kernel(halves), "shh", shape((halves, count, width), f32),
        [
            pltpu.VMEM((pixels, chans), bf16), pltpu.VMEM((chans, width), bf16),
            pltpu.SemaphoreType.DMA((2,)),
        ],
        tap_flops, tap_bytes, vmem=56,
    )(place, feat, w_point)
    own_point, came_point = reduce_ch(main)
    halos, local_sums, edges = ([None] * len(groups) for _ in range(3))

    def tap_scratch(number):
        return [pltpu.VMEM((number, chans, width), bf16), pltpu.SemaphoreType.DMA((number,))]

    def side_call(number, builds):
        branches, spots, group_cols = groups[number]
        shapes = [
            shape((len(branches), rows, cols, width), f32),
            shape((halves, 2, part, group_cols, width), f32),
        ]
        scratch = [pltpu.VMEM((rows, cols, 2 * width), f32), *tap_scratch(6 * len(branches))]
        if builds:
            shapes.append(tall_shape)
            scratch.append(pltpu.SemaphoreType.DMA)
        return call(
            side_kernel(rows, cols, halves, branches, spots, builds),
            "shvh" if builds else "svh", tuple(shapes), scratch,
            6 * len(branches) * tap_flops, 6 * len(branches) * tap_bytes, vmem=44,
        )

    local_sums[1], halo, tall = side_call(1, True)(place, feat, other, taps)
    halos[1] = reduce_ch(halo)
    came_point = after(came_point, tall)
    local_sums[0], halo = side_call(0, False)(place, after(tall, came_point, *gone), taps)
    halos[0] = reduce_ch(halo)

    def send_halo(number, *earlier):
        own, came = halos[number]
        came = after(came, *earlier)
        halo_sum = (own + came.astype(f32)).astype(wire)
        edges[number] = (to_right(halo_sum[1]), to_left(halo_sum[0]))
        return halo_sum

    sent = send_halo(1, halo)
    main = call(
        centre_kernel(rows, cols, halves), "svh" + "v" * len(groups),
        shape((halves, count, 3 * width), f32),
        [pltpu.VMEM((rows, cols, width), f32), *tap_scratch(9)],
        9 * tap_flops, 9 * tap_bytes, vmem=44,
    )(place, after(tall, sent), taps, *local_sums)
    own, came = reduce_ch(main)
    send_halo(0, main)

    pixel = jnp.arange(pixels, dtype=jnp.int32)
    labels, tile_list = lax.optimization_barrier((labels, tile_list, main))[:2]
    active = jnp.any(tile_list.reshape(1, -1) == (pixel // 128)[:, None], axis=1).astype(f32)
    first = ch * count if halves == 2 else 0
    label_part = lax.dynamic_slice(labels.reshape(pixels, 1), (first, 0), (count, 1))
    active_part = lax.dynamic_slice(active.reshape(pixels, 1), (first, 0), (count, 1))

    edge_shape = shape((part, halo_cols, width), bf16)
    head_field = pltpu.VMEM((part, cols, 4 * width), f32)
    operands = (
        own_point, came_point.astype(f32), own, came.astype(f32),
        *(e.astype(f32) for pair in edges for e in pair),
        label_part, active_part,
        branch_scale.reshape(1, -1), branch_shift.reshape(1, -1), w_proj,
        proj_scale.reshape(1, -1), proj_shift.reshape(1, -1), w_class,
    )
    d_point, d_side, edge_left, edge_right = call(
        head_kernel(part, cols, width), "s" + "v" * len(operands),
        (
            shape((part, cols, width), bf16), shape((part, cols, 3 * width), bf16),
            edge_shape, edge_shape,
        ),
        [head_field, head_field],
        2 * count * width * (8 * width + 2 * w_class.shape[1]), 32 * count * width,
    )(place, *operands)

    acc_shape = shape((rows, cols, chans), f32)
    out_shape = shape((rows, cols, chans), bf16)

    def local_taps(d, mine, acc):
        body = back_local_kernel(rows, cols, width, halves, mine, acc is None)
        operands = (d, swap_lat(d), taps) + (() if acc is None else (acc,))
        return call(
            body, "svvh" + "v" * (len(operands) - 3), acc_shape,
            [
                pltpu.VMEM((6, part * cols, 3 * width), bf16), pltpu.VMEM(taps.shape, bf16),
                pltpu.SemaphoreType.DMA((3,)),
            ],
            14 * tap_flops, 14 * tap_bytes, vmem=44,
        )(place, *operands)

    def halo_taps(halo, mine, acc, last):
        body = back_halo_kernel(rows, cols, width, halves, mine, last)
        operands = (halo, swap_lat(halo), w_point, taps, acc)
        return call(
            body, "svvvhv", out_shape if last else acc_shape,
            [
                pltpu.VMEM((6, part * cols, 2 * width), bf16), pltpu.VMEM(taps.shape, bf16),
                pltpu.SemaphoreType.DMA((3, 3, 3)),
            ]
            + [pltpu.VMEM((rows, cols, chans), f32)] * last,
            5 * tap_flops, 14 * tap_bytes, vmem=44,
        )(place, *operands)

    left, right = to_right(edge_right), to_left(edge_left)
    acc = local_taps(d_side, True, None)
    halo_mine = jnp.concatenate([after(left, acc), right, d_point], 1)
    if halves == 2:
        d_came = after(swap_ch(d_side), acc)
        halo_came = swap_ch(halo_mine)
        acc = halo_taps(halo_mine, True, acc, False)
        acc = local_taps(d_came, False, acc)
        return halo_taps(after(halo_came, acc), False, acc, True)
    return halo_taps(halo_mine, True, acc, True)


def solution(mesh):
    placed = (
        P("lat", "lon", "ch"),
        P("lat", "lon"),
        P("lat", "lon", None),
        P("ch", None),
        P(None, None, "ch", None),
        P(),
        P(),
        P(),
        P(),
        P(),
        P(),
    )
    return jax.shard_map(
        local, mesh=mesh, in_specs=placed, out_specs=P("lat", "lon", "ch"), check_vma=False
    )
```

```python
import functools

import jax
import jax.numpy as jnp
from jax import lax
from jax.experimental import pallas as pl
from jax.experimental.pallas import tpu as pltpu
from jax.sharding import PartitionSpec as P

atrous_rates = (6, 12, 18)
f32 = jnp.float32
bf16 = jnp.bfloat16
wire = jnp.float16
mebi = 1024 * 1024
groups = (((2, 0), (0, 18), 24), ((1,), (0,), 12))
halo_at = (30, 18, 0)
halo_cols = 36


def mul(lhs, rhs):
    return jnp.dot(lhs, rhs, preferred_element_type=f32)


def mul_t(lhs, rhs):
    return lax.dot_general(lhs, rhs, (((1,), (1,)), ((), ())), preferred_element_type=f32)


def call(body, kinds, out_shape, scratch, flops, moved, vmem=16):
    space = {"s": pltpu.SMEM, "v": pltpu.VMEM, "h": pltpu.HBM}
    return pl.pallas_call(
        body,
        in_specs=[pl.BlockSpec(memory_space=space[k]) for k in kinds],
        out_specs=jax.tree.map(lambda _: pl.BlockSpec(memory_space=pltpu.VMEM), out_shape),
        out_shape=out_shape,
        scratch_shapes=scratch,
        compiler_params=pltpu.CompilerParams(vmem_limit_bytes=vmem * mebi),
        cost_estimate=pl.CostEstimate(
            flops=flops // 16, bytes_accessed=moved // 16, transcendentals=0
        ),
    )


def shape(dims, kind):
    return jax.ShapeDtypeStruct(dims, kind)


def slot_of(half, halves, ch):
    return 0 if halves == 1 else (ch if half else 1 - ch)


def beside(*values):
    return values[0] if len(values) == 1 else jnp.concatenate(values, 1)


def point_kernel():
    def body(feat, point, taps, out, feat_held, taps_held, point_held, arrived):
        copies = [
            pltpu.make_async_copy(feat, feat_held, arrived.at[0]),
            pltpu.make_async_copy(point, point_held, arrived.at[1]),
            pltpu.make_async_copy(taps, taps_held, arrived.at[2]),
        ]
        for copy in copies:
            copy.start()
        copies[0].wait()
        copies[1].wait()
        out[...] = mul(feat_held[...], point_held[...])
        copies[2].wait()

    return body


def column_steps(total, tall, taps, branch, cols_of, rows, cols):
    pixels, cut = rows * cols, atrous_rates[branch] * cols

    def row_step(u):
        start = pixels + (u - 1) * cut
        return mul(tall[start : start + pixels, :], beside(*(taps[branch, u, v] for v in cols_of)))

    total[...] = (row_step(0) + row_step(1) + row_step(2)).reshape(total.shape)


def side_kernel(rows, cols, halves, branches, spots, builds):
    part, pixels = rows // halves, rows * cols

    def body(place, *refs):
        if builds:
            feat, other, taps, local_sum, halo, tall, total = refs
        else:
            tall, taps, local_sum, halo, total = refs
        lat, ch = place[0], place[1]
        width = total.shape[-1] // 2
        if builds:
            spot = pl.multiple_of((1 - lat) * (2 * pixels), pixels)
            blank = pl.multiple_of(lat * (2 * pixels), pixels)
            tall[pixels : 2 * pixels, :] = feat[...]
            tall[pl.ds(spot, pixels), :] = other[...]
            tall[pl.ds(blank, pixels), :] = jnp.zeros((pixels, tall.shape[1]), bf16)
        for index, (branch, at) in enumerate(zip(branches, spots)):
            rate = atrous_rates[branch]
            column_steps(total, tall, taps, branch, (0, 2), rows, cols)
            for half in range(halves):
                slot, its = slot_of(half, halves, ch), slice(half * part, (half + 1) * part)
                halo[slot, 1, :, at : at + rate, :] = total[its, cols - rate :, :width]
                halo[slot, 0, :, at : at + rate, :] = total[its, :rate, width:]
            local_sum[index, :, rate:, :] = total[:, : cols - rate, :width]
            local_sum[index, :, :rate, :] = jnp.zeros((rows, rate, width), f32)
            local_sum[index, :, : cols - rate, :] += total[:, rate:, width:]

    return body


def centre_kernel(rows, cols, halves):
    part = rows // halves

    def body(place, tall, taps, point_sum, *refs):
        local_sums, (out, total) = refs[: len(groups)], refs[len(groups) :]
        width = total.shape[-1]

        def store(value, lane):
            for half in range(halves):
                its = slice(half * part, (half + 1) * part)
                out[slot_of(half, halves, place[1]), :, lane * width : (lane + 1) * width] = value(
                    its
                ).reshape(part * cols, width)

        store(lambda its: point_sum[its.start * cols : its.stop * cols, :], 0)
        for number, (branches, _, _) in enumerate(groups):
            for index, branch in enumerate(branches):
                column_steps(total, tall, taps, branch, (1,), rows, cols)
                store(lambda its: total[its] + local_sums[number][index, its], branch + 1)

    return body


def head_kernel(rows, cols, width):
    pixels = rows * cols

    def body(
        place, own, came, left_a, right_a, left_b, right_b,
        labels, active, scales, shifts, w_proj, proj_scale, proj_shift, w_class,
        d_point, d_side, to_left, to_right, total, grad,
    ):
        total[...] = (own[...] + came[...]).reshape(total.shape)
        edges = ((left_a, right_a), (left_b, right_b))
        for (branches, spots, _), (left, right) in zip(groups, edges):
            for branch, at in zip(branches, spots):
                rate = atrous_rates[branch]
                lanes = slice((branch + 1) * width, (branch + 2) * width)
                total[:, :rate, lanes] += left[:, at : at + rate, :]
                total[:, cols - rate :, lanes] += right[:, at : at + rate, :]
        scale = beside(*(scales[k : k + 1, :] for k in range(4)))
        shift = beside(*(shifts[k : k + 1, :] for k in range(4)))
        pre = total[...].reshape(pixels, 4 * width) * scale + shift
        joined = jnp.maximum(pre, 0.0).astype(bf16)
        z_pre = mul(joined, w_proj[...]) * proj_scale[...] + proj_shift[...]
        hidden = jnp.maximum(z_pre, 0.0).astype(bf16)
        logits = mul(hidden, w_class[...])
        expo = jnp.exp(logits - jnp.max(logits, axis=1, keepdims=True))
        prob = expo / jnp.sum(expo, axis=1, keepdims=True)
        ids = lax.broadcasted_iota(jnp.int32, prob.shape, 1)
        onehot = jnp.where(ids == labels[...], 1.0, 0.0)
        d_logits = (active[...] * (prob - onehot)).astype(bf16)
        d_hidden = mul_t(d_logits, w_class[...]) * proj_scale[...]
        d_z = jnp.where(z_pre > 0, d_hidden, 0.0).astype(bf16)
        d_joined = mul_t(d_z, w_proj[...]) * scale
        grad[...] = jnp.where(pre > 0, d_joined, 0.0).reshape(grad.shape)
        d_point[...] = grad[:, :, :width].astype(bf16)
        d_side[...] = grad[:, :, width:].astype(bf16)
        for branch, rate in enumerate(atrous_rates):
            at, lanes = halo_at[branch], slice((branch + 1) * width, (branch + 2) * width)
            to_left[:, at : at + rate, :] = grad[:, :rate, lanes].astype(bf16)
            to_right[:, at : at + rate, :] = grad[:, cols - rate :, lanes].astype(bf16)

    return body


def spread(
    total, field, taps, branch, steps, begin, same_band, lat, rows, part, cols
):
    rate = atrous_rates[branch]

    def add(source, target, count, u):
        weights = beside(*(taps[branch, u, v] for v in steps))
        lhs = field[pl.ds(pl.multiple_of(source * cols, cols), count * cols), :]
        product = mul_t(lhs[:, : len(steps) * weights.shape[1] // len(steps)], weights)
        total[pl.ds(target, count)] += product.reshape(count, cols, product.shape[1])

    if same_band:
        first = begin == 0
        add(0, begin, part, 1)
        inward = min(part, rows - rate)
        add(
            jnp.where(first, 0, part - inward),
            jnp.where(first, rate, rows - inward - rate),
            inward,
            jnp.where(first, 2, 0),
        )
        if part > rate:
            outward = part - rate
            add(
                jnp.where(first, rate, 0),
                jnp.where(first, 0, rows - outward),
                outward,
                jnp.where(first, 0, 2),
            )
    else:
        u = 2 * lat
        near, far = min(rate, part), rate - part
        is_near = (begin == 0) == (lat == 0) if part < rows else True

        def near_rows():
            add(lat * (part - near), (1 - lat) * (rows - rate) + lat * (rate - near), near, u)

        if part == rows:
            near_rows()
        else:
            pl.when(is_near)(near_rows)
            if far > 0:

                @pl.when(jnp.logical_not(is_near))
                def _():
                    add(lat * (part - far), (1 - lat) * (rows - rate + part), far, u)


back_order = (2, 1, 0)


def back_local_kernel(rows, cols, width, halves, mine, first):
    part = rows // halves

    def body(place, own, other, taps, *refs):
        copies = {}
        if first:
            all_taps, (total, taps, fields, arrived) = taps, refs
            copies = {
                b: pltpu.make_async_copy(all_taps.at[b], taps.at[b], arrived.at[b])
                for b in back_order
            }
            for copy in copies.values():
                copy.start()
        else:
            acc, total, fields = refs
        lat, ch = place[0], place[1]
        begin = 0 if halves == 1 else (ch if mine else 1 - ch) * part
        total[...] = jnp.zeros_like(total) if first else acc[...]
        for branch in back_order:
            rate = atrous_rates[branch]
            lanes = slice(branch * width, (branch + 1) * width)
            for source, same_band in ((own, True), (other, False)):
                field = fields.at[2 * branch + same_band]
                value = source[:, :, lanes].astype(f32)
                zeros = jnp.zeros((part, rate, width), f32)
                left = jnp.concatenate([value[:, rate:, :], zeros], 1)
                right = jnp.concatenate([zeros, value[:, : cols - rate, :]], 1)
                for step, shifted in enumerate((left, value, right)):
                    field[:, step * width : (step + 1) * width] = shifted.reshape(
                        part * cols, width
                    ).astype(bf16)
                if first and same_band:
                    copies[branch].wait()
                spread(
                    total, field, taps, branch, (0, 1, 2), begin, same_band,
                    lat, rows, part, cols,
                )

    return body


def back_halo_kernel(rows, cols, width, halves, mine, last):
    part = rows // halves

    def body(place, own, other, taps, point, acc, out, fields, *refs):
        lat, ch = place[0], place[1]
        begin = 0 if halves == 1 else (ch if mine else 1 - ch) * part
        total = refs[0] if last else out
        total[...] = acc[...]
        block = own[:, 2 * halo_cols :, :].reshape(part * cols, width)
        product = mul_t(block, point[...])
        total[pl.ds(begin, part)] += product.reshape(part, cols, product.shape[1])
        for branch in back_order:
            rate, at = atrous_rates[branch], halo_at[branch]
            for source, same_band in ((own, True), (other, False)):
                field = fields.at[2 * branch + same_band]
                left = source[:, at : at + rate, :].astype(f32)
                right = source[:, halo_cols + at : halo_cols + at + rate, :].astype(f32)
                zeros = jnp.zeros((part, cols - rate, width), f32)
                for step, value in enumerate(
                    (jnp.concatenate([left, zeros], 1), jnp.concatenate([zeros, right], 1))
                ):
                    field[:, step * width : (step + 1) * width] = value.reshape(
                        part * cols, width
                    ).astype(bf16)
                spread(
                    total, field, taps, branch, (2, 0), begin, same_band,
                    lat, rows, part, cols,
                )
        if last:
            out[...] = total[...].astype(bf16)

    return body


def shift_pairs(size, step):
    return [(i, (i + step) % size) for i in range(size)]


def after(value, *first):
    return lax.optimization_barrier((value, *first))[0]


def local(
    features, labels, tile_list, w_point, w_rates, branch_scale, branch_shift,
    w_proj, proj_scale, proj_shift, w_class,
):
    rows, cols, chans = features.shape
    pixels = rows * cols
    width = w_point.shape[1]
    lon_size, ch_size, lat_size = (lax.axis_size(a) for a in ("lon", "ch", "lat"))
    assert lat_size == 2 and max(atrous_rates) <= min(rows, cols)
    halves = 2 if ch_size == 2 else 1
    part = rows // halves
    count = pixels // halves
    lat, ch = lax.axis_index("lat"), lax.axis_index("ch")
    place = jnp.stack([lat, ch]).astype(jnp.int32)
    taps = w_rates.reshape(3, 3, 3, chans, width)
    tap_flops = 2 * pixels * chans * width
    tap_bytes = 2 * chans * width

    def swap_lat(value):
        return lax.ppermute(value, "lat", shift_pairs(2, 1))

    def swap_ch(value):
        return lax.ppermute(value, "ch", shift_pairs(2, 1))

    def to_left(value):
        return lax.ppermute(value, "lon", shift_pairs(lon_size, -1))

    def to_right(value):
        return lax.ppermute(value, "lon", shift_pairs(lon_size, 1))

    gone = []

    def reduce_ch(parts):
        if halves == 2:
            sent = parts[0].astype(wire)
            gone.append(sent)
            return parts[1], swap_ch(sent)
        own = lax.psum(parts[0], "ch")
        return own, jnp.zeros(own.shape, wire)

    feat = features.reshape(pixels, chans)
    other = swap_lat(feat)
    tall_shape = shape((3 * pixels, chans), bf16)

    halos, local_sums, edges = ([None] * len(groups) for _ in range(3))

    point_sum, feat_held, taps_held = call(
        point_kernel(), "hhh",
        (
            shape((pixels, width), f32), shape((pixels, chans), bf16), shape(taps.shape, bf16),
        ),
        [pltpu.VMEM((chans, width), bf16), pltpu.SemaphoreType.DMA((3,))],
        tap_flops, 27 * tap_bytes, vmem=36,
    )(feat, w_point, taps)
    other = after(other, point_sum)

    def side_call(number, builds):
        branches, spots, group_cols = groups[number]
        shapes = [
            shape((len(branches), rows, cols, width), f32),
            shape((halves, 2, part, group_cols, width), f32),
        ]
        if builds:
            shapes.append(tall_shape)
        return call(
            side_kernel(rows, cols, halves, branches, spots, builds),
            "svvv" if builds else "svv", tuple(shapes), [pltpu.VMEM((rows, cols, 2 * width), f32)],
            6 * len(branches) * tap_flops, 6 * len(branches) * tap_bytes,
        )

    local_sums[1], halo, tall = side_call(1, True)(place, feat_held, other, taps_held)
    halos[1] = reduce_ch(halo)
    local_sums[0], halo = side_call(0, False)(place, after(tall, *gone), taps_held)
    halos[0] = reduce_ch(halo)

    def send_halo(number, *earlier):
        own, came = halos[number]
        came = after(came, *earlier)
        halo_sum = (own + came.astype(f32)).astype(wire)
        edges[number] = (to_right(halo_sum[1]), to_left(halo_sum[0]))
        return halo_sum

    sent = send_halo(1, halo)
    main = call(
        centre_kernel(rows, cols, halves), "svvv" + "v" * len(groups),
        shape((halves, count, 4 * width), f32), [pltpu.VMEM((rows, cols, width), f32)],
        10 * tap_flops, 10 * tap_bytes,
    )(place, after(tall, sent), taps_held, point_sum, *local_sums)
    own, came = reduce_ch(main)
    send_halo(0, main)

    pixel = jnp.arange(pixels, dtype=jnp.int32)
    labels, tile_list = lax.optimization_barrier((labels, tile_list, main))[:2]
    active = jnp.any(tile_list.reshape(1, -1) == (pixel // 128)[:, None], axis=1).astype(f32)
    first = ch * count if halves == 2 else 0
    label_part = lax.dynamic_slice(labels.reshape(pixels, 1), (first, 0), (count, 1))
    active_part = lax.dynamic_slice(active.reshape(pixels, 1), (first, 0), (count, 1))

    edge_shape = shape((part, halo_cols, width), bf16)
    head_field = pltpu.VMEM((part, cols, 4 * width), f32)
    operands = (
        own, came.astype(f32),
        *(e.astype(f32) for pair in edges for e in pair),
        label_part, active_part,
        branch_scale, branch_shift, w_proj,
        proj_scale.reshape(1, -1), proj_shift.reshape(1, -1), w_class,
    )
    d_point, d_side, edge_left, edge_right = call(
        head_kernel(part, cols, width), "s" + "v" * len(operands),
        (
            shape((part, cols, width), bf16), shape((part, cols, 3 * width), bf16),
            edge_shape, edge_shape,
        ),
        [head_field, head_field],
        2 * count * width * (8 * width + 2 * w_class.shape[1]), 32 * count * width,
    )(place, *operands)

    acc_shape = shape((rows, cols, chans), f32)
    out_shape = shape((rows, cols, chans), bf16)

    fields = pltpu.VMEM((6, part * cols, 3 * width), bf16)
    acc, back_taps = call(
        back_local_kernel(rows, cols, width, halves, True, True), "svvh",
        (acc_shape, shape(taps.shape, bf16)), [fields, pltpu.SemaphoreType.DMA((3,))],
        14 * tap_flops, 14 * tap_bytes, vmem=36,
    )(place, d_side, swap_lat(d_side), taps)

    def halo_taps(halo, mine, acc, last):
        return call(
            back_halo_kernel(rows, cols, width, halves, mine, last),
            "svvvvv", out_shape if last else acc_shape,
            [pltpu.VMEM((6, part * cols, 2 * width), bf16)]
            + [pltpu.VMEM((rows, cols, chans), f32)] * last,
            5 * tap_flops, 14 * tap_bytes,
        )(place, halo, swap_lat(halo), back_taps, w_point, acc)

    left, right = to_right(edge_right), to_left(edge_left)
    halo_mine = jnp.concatenate([after(left, acc), right, d_point], 1)
    if halves == 2:
        d_came = after(swap_ch(d_side), acc)
        halo_came = swap_ch(halo_mine)
        acc = halo_taps(halo_mine, True, acc, False)
        acc = call(
            back_local_kernel(rows, cols, width, halves, False, False), "svvvv", acc_shape,
            [fields], 14 * tap_flops, 14 * tap_bytes,
        )(place, d_came, swap_lat(d_came), back_taps, acc)
        return halo_taps(after(halo_came, acc), False, acc, True)
    return halo_taps(halo_mine, True, acc, True)


def solution(mesh):
    placed = (
        P("lat", "lon", "ch"),
        P("lat", "lon"),
        P("lat", "lon", None),
        P("ch", None),
        P(None, None, "ch", None),
        P(),
        P(),
        P(),
        P(),
        P(),
        P(),
    )
    return jax.shard_map(
        local, mesh=mesh, in_specs=placed, out_specs=P("lat", "lon", "ch"), check_vma=False
    )
```

```python
import functools

import jax
import jax.numpy as jnp
from jax import lax
from jax.experimental import pallas as pl
from jax.experimental.pallas import tpu as pltpu
from jax.sharding import PartitionSpec as P

atrous_rates = (6, 12, 18)
f32 = jnp.float32
bf16 = jnp.bfloat16
wire = jnp.float16
mebi = 1024 * 1024
groups = (((2, 0), (0, 18), 24), ((1,), (0,), 12))
halo_at = (30, 18, 0)
halo_cols = 36


def mul(lhs, rhs):
    return jnp.dot(lhs, rhs, preferred_element_type=f32)


def mul_t(lhs, rhs):
    return lax.dot_general(lhs, rhs, (((1,), (1,)), ((), ())), preferred_element_type=f32)


def call(body, kinds, out_shape, scratch, flops, moved, vmem=16):
    space = {"s": pltpu.SMEM, "v": pltpu.VMEM, "h": pltpu.HBM}
    return pl.pallas_call(
        body,
        in_specs=[pl.BlockSpec(memory_space=space[k]) for k in kinds],
        out_specs=jax.tree.map(lambda _: pl.BlockSpec(memory_space=pltpu.VMEM), out_shape),
        out_shape=out_shape,
        scratch_shapes=scratch,
        compiler_params=pltpu.CompilerParams(vmem_limit_bytes=vmem * mebi),
        cost_estimate=pl.CostEstimate(
            flops=flops // 16, bytes_accessed=moved // 16, transcendentals=0
        ),
    )


def shape(dims, kind):
    return jax.ShapeDtypeStruct(dims, kind)


def slot_of(half, halves, ch):
    return 0 if halves == 1 else (ch if half else 1 - ch)


def beside(*values):
    return values[0] if len(values) == 1 else jnp.concatenate(values, 1)


def point_kernel():
    def body(feat, point, taps, out, feat_held, taps_held, point_held, arrived):
        copies = [
            pltpu.make_async_copy(feat, feat_held, arrived.at[0]),
            pltpu.make_async_copy(point, point_held, arrived.at[1]),
            pltpu.make_async_copy(taps, taps_held, arrived.at[2]),
        ]
        for copy in copies:
            copy.start()
        copies[0].wait()
        copies[1].wait()
        out[...] = mul(feat_held[...], point_held[...])
        copies[2].wait()

    return body


def column_steps(total, tall, taps, branch, cols_of, rows, cols):
    pixels, cut = rows * cols, atrous_rates[branch] * cols

    def row_step(u):
        start = pixels + (u - 1) * cut
        return mul(tall[start : start + pixels, :], beside(*(taps[branch, u, v] for v in cols_of)))

    total[...] = (row_step(0) + row_step(1) + row_step(2)).reshape(total.shape)


def side_kernel(rows, cols, halves, branches, spots, builds):
    part, pixels = rows // halves, rows * cols

    def body(place, *refs):
        if builds:
            feat, other, taps, local_sum, halo, tall, total = refs
        else:
            tall, taps, local_sum, halo, total = refs
        lat, ch = place[0], place[1]
        width = total.shape[-1] // 2
        if builds:
            spot = pl.multiple_of((1 - lat) * (2 * pixels), pixels)
            blank = pl.multiple_of(lat * (2 * pixels), pixels)
            tall[pixels : 2 * pixels, :] = feat[...]
            tall[pl.ds(spot, pixels), :] = other[...]
            tall[pl.ds(blank, pixels), :] = jnp.zeros((pixels, tall.shape[1]), bf16)
        for index, (branch, at) in enumerate(zip(branches, spots)):
            rate = atrous_rates[branch]
            column_steps(total, tall, taps, branch, (0, 2), rows, cols)
            for half in range(halves):
                slot, its = slot_of(half, halves, ch), slice(half * part, (half + 1) * part)
                halo[slot, 1, :, at : at + rate, :] = total[its, cols - rate :, :width]
                halo[slot, 0, :, at : at + rate, :] = total[its, :rate, width:]
            local_sum[index, :, rate:, :] = total[:, : cols - rate, :width]
            local_sum[index, :, :rate, :] = jnp.zeros((rows, rate, width), f32)
            local_sum[index, :, : cols - rate, :] += total[:, rate:, width:]

    return body


def centre_kernel(rows, cols, halves):
    part = rows // halves

    def body(place, tall, taps, point_sum, *refs):
        local_sums, (out, total) = refs[: len(groups)], refs[len(groups) :]
        width = total.shape[-1]

        def store(value, lane):
            for half in range(halves):
                its = slice(half * part, (half + 1) * part)
                out[slot_of(half, halves, place[1]), :, lane * width : (lane + 1) * width] = value(
                    its
                ).reshape(part * cols, width)

        store(lambda its: point_sum[its.start * cols : its.stop * cols, :], 0)
        for number, (branches, _, _) in enumerate(groups):
            for index, branch in enumerate(branches):
                column_steps(total, tall, taps, branch, (1,), rows, cols)
                store(lambda its: total[its] + local_sums[number][index, its], branch + 1)

    return body


def head_kernel(rows, cols, width):
    pixels = rows * cols

    def body(
        place, own, came, left_a, right_a, left_b, right_b,
        labels, active, scales, shifts, w_proj, proj_scale, proj_shift, w_class,
        d_point, d_side, to_left, to_right, total, grad,
    ):
        total[...] = (own[...] + came[...]).reshape(total.shape)
        edges = ((left_a, right_a), (left_b, right_b))
        for (branches, spots, _), (left, right) in zip(groups, edges):
            for branch, at in zip(branches, spots):
                rate = atrous_rates[branch]
                lanes = slice((branch + 1) * width, (branch + 2) * width)
                total[:, :rate, lanes] += left[:, at : at + rate, :]
                total[:, cols - rate :, lanes] += right[:, at : at + rate, :]
        scale = beside(*(scales[k : k + 1, :] for k in range(4)))
        shift = beside(*(shifts[k : k + 1, :] for k in range(4)))
        pre = total[...].reshape(pixels, 4 * width) * scale + shift
        joined = jnp.maximum(pre, 0.0).astype(bf16)
        z_pre = mul(joined, w_proj[...]) * proj_scale[...] + proj_shift[...]
        hidden = jnp.maximum(z_pre, 0.0).astype(bf16)
        logits = mul(hidden, w_class[...])
        expo = jnp.exp(logits - jnp.max(logits, axis=1, keepdims=True))
        prob = expo / jnp.sum(expo, axis=1, keepdims=True)
        ids = lax.broadcasted_iota(jnp.int32, prob.shape, 1)
        onehot = jnp.where(ids == labels[...], 1.0, 0.0)
        d_logits = (active[...] * (prob - onehot)).astype(bf16)
        d_hidden = mul_t(d_logits, w_class[...]) * proj_scale[...]
        d_z = jnp.where(z_pre > 0, d_hidden, 0.0).astype(bf16)
        d_joined = mul_t(d_z, w_proj[...]) * scale
        grad[...] = jnp.where(pre > 0, d_joined, 0.0).reshape(grad.shape)
        d_point[...] = grad[:, :, :width].astype(bf16)
        d_side[...] = grad[:, :, width:].astype(bf16)
        for branch, rate in enumerate(atrous_rates):
            at, lanes = halo_at[branch], slice((branch + 1) * width, (branch + 2) * width)
            to_left[:, at : at + rate, :] = grad[:, :rate, lanes].astype(bf16)
            to_right[:, at : at + rate, :] = grad[:, cols - rate :, lanes].astype(bf16)

    return body


def spread(
    total, field, taps, branch, steps, begin, same_band, lat, rows, part, cols
):
    rate = atrous_rates[branch]

    def add(source, target, count, u):
        weights = beside(*(taps[branch, u, v] for v in steps))
        lhs = field[pl.ds(pl.multiple_of(source * cols, cols), count * cols), :]
        product = mul_t(lhs[:, : len(steps) * weights.shape[1] // len(steps)], weights)
        total[pl.ds(target, count)] += product.reshape(count, cols, product.shape[1])

    if same_band:
        first = begin == 0
        add(0, begin, part, 1)
        inward = min(part, rows - rate)
        add(
            jnp.where(first, 0, part - inward),
            jnp.where(first, rate, rows - inward - rate),
            inward,
            jnp.where(first, 2, 0),
        )
        if part > rate:
            outward = part - rate
            add(
                jnp.where(first, rate, 0),
                jnp.where(first, 0, rows - outward),
                outward,
                jnp.where(first, 0, 2),
            )
    else:
        u = 2 * lat
        near, far = min(rate, part), rate - part
        is_near = (begin == 0) == (lat == 0) if part < rows else True

        def near_rows():
            add(lat * (part - near), (1 - lat) * (rows - rate) + lat * (rate - near), near, u)

        if part == rows:
            near_rows()
        else:
            pl.when(is_near)(near_rows)
            if far > 0:

                @pl.when(jnp.logical_not(is_near))
                def _():
                    add(lat * (part - far), (1 - lat) * (rows - rate + part), far, u)


back_order = (2, 1, 0)


def back_local_kernel(rows, cols, width, halves, mine, first):
    part = rows // halves

    def body(place, own, other, taps, *refs):
        copies = {}
        if first:
            all_taps, (total, taps, fields, arrived) = taps, refs
            copies = {
                b: pltpu.make_async_copy(all_taps.at[b], taps.at[b], arrived.at[b])
                for b in back_order
            }
            for copy in copies.values():
                copy.start()
        else:
            acc, total, fields = refs
        lat, ch = place[0], place[1]
        begin = 0 if halves == 1 else (ch if mine else 1 - ch) * part
        total[...] = jnp.zeros_like(total) if first else acc[...]
        for branch in back_order:
            rate = atrous_rates[branch]
            lanes = slice(branch * width, (branch + 1) * width)
            for source, same_band in ((own, True), (other, False)):
                field = fields.at[2 * branch + same_band]
                value = source[:, :, lanes].astype(f32)
                zeros = jnp.zeros((part, rate, width), f32)
                left = jnp.concatenate([value[:, rate:, :], zeros], 1)
                right = jnp.concatenate([zeros, value[:, : cols - rate, :]], 1)
                for step, shifted in enumerate((left, value, right)):
                    field[:, step * width : (step + 1) * width] = shifted.reshape(
                        part * cols, width
                    ).astype(bf16)
                if first and same_band:
                    copies[branch].wait()
                spread(
                    total, field, taps, branch, (0, 1, 2), begin, same_band,
                    lat, rows, part, cols,
                )

    return body


def back_halo_kernel(rows, cols, width, halves, mine, bands, last):
    part = rows // halves

    def body(place, own, other, taps, point, acc, out, fields, *refs):
        lat, ch = place[0], place[1]
        begin = 0 if halves == 1 else (ch if mine else 1 - ch) * part
        total = refs[0] if last else out
        total[...] = acc[...]
        if True in bands:
            block = own[:, 2 * halo_cols :, :].reshape(part * cols, width)
            product = mul_t(block, point[...])
            total[pl.ds(begin, part)] += product.reshape(part, cols, product.shape[1])
        for branch in back_order:
            rate, at = atrous_rates[branch], halo_at[branch]
            for same_band in bands:
                source = own if same_band else other
                field = fields.at[2 * branch + same_band]
                left = source[:, at : at + rate, :].astype(f32)
                right = source[:, halo_cols + at : halo_cols + at + rate, :].astype(f32)
                zeros = jnp.zeros((part, cols - rate, width), f32)
                for step, value in enumerate(
                    (jnp.concatenate([left, zeros], 1), jnp.concatenate([zeros, right], 1))
                ):
                    field[:, step * width : (step + 1) * width] = value.reshape(
                        part * cols, width
                    ).astype(bf16)
                spread(
                    total, field, taps, branch, (2, 0), begin, same_band,
                    lat, rows, part, cols,
                )
        if last:
            out[...] = total[...].astype(bf16)

    return body


def shift_pairs(size, step):
    return [(i, (i + step) % size) for i in range(size)]


def after(value, *first):
    return lax.optimization_barrier((value, *first))[0]


def local(
    features, labels, tile_list, w_point, w_rates, branch_scale, branch_shift,
    w_proj, proj_scale, proj_shift, w_class,
):
    rows, cols, chans = features.shape
    pixels = rows * cols
    width = w_point.shape[1]
    lon_size, ch_size, lat_size = (lax.axis_size(a) for a in ("lon", "ch", "lat"))
    assert lat_size == 2 and max(atrous_rates) <= min(rows, cols)
    halves = 2 if ch_size == 2 else 1
    part = rows // halves
    count = pixels // halves
    lat, ch = lax.axis_index("lat"), lax.axis_index("ch")
    place = jnp.stack([lat, ch]).astype(jnp.int32)
    taps = w_rates.reshape(3, 3, 3, chans, width)
    tap_flops = 2 * pixels * chans * width
    tap_bytes = 2 * chans * width

    def swap_lat(value):
        return lax.ppermute(value, "lat", shift_pairs(2, 1))

    def swap_ch(value):
        return lax.ppermute(value, "ch", shift_pairs(2, 1))

    def to_left(value):
        return lax.ppermute(value, "lon", shift_pairs(lon_size, -1))

    def to_right(value):
        return lax.ppermute(value, "lon", shift_pairs(lon_size, 1))

    gone = []

    def reduce_ch(parts):
        if halves == 2:
            sent = parts[0].astype(wire)
            gone.append(sent)
            return parts[1], swap_ch(sent)
        own = lax.psum(parts[0], "ch")
        return own, jnp.zeros(own.shape, wire)

    feat = features.reshape(pixels, chans)
    other = swap_lat(feat)
    tall_shape = shape((3 * pixels, chans), bf16)

    halos, local_sums, edges = ([None] * len(groups) for _ in range(3))

    point_sum, feat_held, taps_held = call(
        point_kernel(), "hhh",
        (
            shape((pixels, width), f32), shape((pixels, chans), bf16), shape(taps.shape, bf16),
        ),
        [pltpu.VMEM((chans, width), bf16), pltpu.SemaphoreType.DMA((3,))],
        tap_flops, 27 * tap_bytes, vmem=36,
    )(feat, w_point, taps)
    other = after(other, point_sum)

    def side_call(number, builds):
        branches, spots, group_cols = groups[number]
        shapes = [
            shape((len(branches), rows, cols, width), f32),
            shape((halves, 2, part, group_cols, width), f32),
        ]
        if builds:
            shapes.append(tall_shape)
        return call(
            side_kernel(rows, cols, halves, branches, spots, builds),
            "svvv" if builds else "svv", tuple(shapes), [pltpu.VMEM((rows, cols, 2 * width), f32)],
            6 * len(branches) * tap_flops, 6 * len(branches) * tap_bytes,
        )

    local_sums[1], halo, tall = side_call(1, True)(place, feat_held, other, taps_held)
    halos[1] = reduce_ch(halo)
    local_sums[0], halo = side_call(0, False)(place, after(tall, *gone), taps_held)
    halos[0] = reduce_ch(halo)

    def send_halo(number, *earlier):
        own, came = halos[number]
        came = after(came, *earlier)
        halo_sum = (own + came.astype(f32)).astype(wire)
        edges[number] = (to_right(halo_sum[1]), to_left(halo_sum[0]))
        return halo_sum

    sent = send_halo(1, halo)
    main = call(
        centre_kernel(rows, cols, halves), "svvv" + "v" * len(groups),
        shape((halves, count, 4 * width), f32), [pltpu.VMEM((rows, cols, width), f32)],
        10 * tap_flops, 10 * tap_bytes,
    )(place, after(tall, sent), taps_held, point_sum, *local_sums)
    own, came = reduce_ch(main)
    send_halo(0, main)

    pixel = jnp.arange(pixels, dtype=jnp.int32)
    labels, tile_list = lax.optimization_barrier((labels, tile_list, main))[:2]
    active = jnp.any(tile_list.reshape(1, -1) == (pixel // 128)[:, None], axis=1).astype(f32)
    first = ch * count if halves == 2 else 0
    label_part = lax.dynamic_slice(labels.reshape(pixels, 1), (first, 0), (count, 1))
    active_part = lax.dynamic_slice(active.reshape(pixels, 1), (first, 0), (count, 1))

    edge_shape = shape((part, halo_cols, width), bf16)
    head_field = pltpu.VMEM((part, cols, 4 * width), f32)
    operands = (
        own, came.astype(f32),
        *(e.astype(f32) for pair in edges for e in pair),
        label_part, active_part,
        branch_scale, branch_shift, w_proj,
        proj_scale.reshape(1, -1), proj_shift.reshape(1, -1), w_class,
    )
    d_point, d_side, edge_left, edge_right = call(
        head_kernel(part, cols, width), "s" + "v" * len(operands),
        (
            shape((part, cols, width), bf16), shape((part, cols, 3 * width), bf16),
            edge_shape, edge_shape,
        ),
        [head_field, head_field],
        2 * count * width * (8 * width + 2 * w_class.shape[1]), 32 * count * width,
    )(place, *operands)

    acc_shape = shape((rows, cols, chans), f32)
    out_shape = shape((rows, cols, chans), bf16)

    fields = pltpu.VMEM((6, part * cols, 3 * width), bf16)
    acc, back_taps = call(
        back_local_kernel(rows, cols, width, halves, True, True), "svvh",
        (acc_shape, shape(taps.shape, bf16)), [fields, pltpu.SemaphoreType.DMA((3,))],
        14 * tap_flops, 14 * tap_bytes, vmem=36,
    )(place, d_side, swap_lat(d_side), taps)

    def halo_taps(halo, other_halo, mine, bands, acc, last):
        return call(
            back_halo_kernel(rows, cols, width, halves, mine, bands, last),
            "svvvvv", out_shape if last else acc_shape,
            [pltpu.VMEM((6, part * cols, 2 * width), bf16)]
            + [pltpu.VMEM((rows, cols, chans), f32)] * last,
            5 * tap_flops, 14 * tap_bytes,
        )(place, halo, other_halo, back_taps, w_point, acc)

    left, right = to_right(edge_right), to_left(edge_left)
    halo_mine = jnp.concatenate([after(left, acc), right, d_point], 1)
    if halves == 2:
        d_came = after(swap_ch(d_side), acc)
        halo_came = swap_ch(halo_mine)
        both = (True, False)
        acc = halo_taps(halo_mine, swap_lat(halo_mine), True, both, acc, False)
        acc = call(
            back_local_kernel(rows, cols, width, halves, False, False), "svvvv", acc_shape,
            [fields], 14 * tap_flops, 14 * tap_bytes,
        )(place, d_came, swap_lat(d_came), back_taps, acc)
        halo_came = after(halo_came, acc)
        other_halo = swap_lat(halo_came)
        acc = halo_taps(halo_came, halo_came, False, (True,), acc, False)
        return halo_taps(halo_came, other_halo, False, (False,), acc, True)
    return halo_taps(halo_mine, swap_lat(halo_mine), True, (True, False), acc, True)


def solution(mesh):
    placed = (
        P("lat", "lon", "ch"),
        P("lat", "lon"),
        P("lat", "lon", None),
        P("ch", None),
        P(None, None, "ch", None),
        P(),
        P(),
        P(),
        P(),
        P(),
        P(),
    )
    return jax.shard_map(
        local, mesh=mesh, in_specs=placed, out_specs=P("lat", "lon", "ch"), check_vma=False
    )
```

```python
import functools

import jax
import jax.numpy as jnp
from jax import lax
from jax.experimental import pallas as pl
from jax.experimental.pallas import tpu as pltpu
from jax.sharding import PartitionSpec as P

atrous_rates = (6, 12, 18)
f32 = jnp.float32
bf16 = jnp.bfloat16
wire = jnp.float16
mebi = 1024 * 1024
groups = (((2, 0), (0, 18), 24), ((1,), (0,), 12))
halo_at = (30, 18, 0)
halo_cols = 36


def mul(lhs, rhs):
    return jnp.dot(lhs, rhs, preferred_element_type=f32)


def mul_t(lhs, rhs):
    return lax.dot_general(lhs, rhs, (((1,), (1,)), ((), ())), preferred_element_type=f32)


def call(body, kinds, out_shape, scratch, flops, moved, vmem=16):
    space = {"s": pltpu.SMEM, "v": pltpu.VMEM, "h": pltpu.HBM}
    return pl.pallas_call(
        body,
        in_specs=[pl.BlockSpec(memory_space=space[k]) for k in kinds],
        out_specs=jax.tree.map(lambda _: pl.BlockSpec(memory_space=pltpu.VMEM), out_shape),
        out_shape=out_shape,
        scratch_shapes=scratch,
        compiler_params=pltpu.CompilerParams(vmem_limit_bytes=vmem * mebi),
        cost_estimate=pl.CostEstimate(
            flops=flops // 16, bytes_accessed=moved // 16, transcendentals=0
        ),
    )


def shape(dims, kind):
    return jax.ShapeDtypeStruct(dims, kind)


def slot_of(half, halves, ch):
    return 0 if halves == 1 else (ch if half else 1 - ch)


def beside(*values):
    return values[0] if len(values) == 1 else jnp.concatenate(values, 1)


def point_kernel():
    def body(feat, point, taps, out, feat_held, taps_held, point_held, arrived):
        copies = [
            pltpu.make_async_copy(feat, feat_held, arrived.at[0]),
            pltpu.make_async_copy(point, point_held, arrived.at[1]),
            pltpu.make_async_copy(taps, taps_held, arrived.at[2]),
        ]
        for copy in copies:
            copy.start()
        copies[0].wait()
        copies[1].wait()
        out[...] = mul(feat_held[...], point_held[...])
        copies[2].wait()

    return body


def column_steps(total, tall, taps, branch, cols_of, rows, cols):
    pixels, cut = rows * cols, atrous_rates[branch] * cols

    def row_step(u):
        start = pixels + (u - 1) * cut
        return mul(tall[start : start + pixels, :], beside(*(taps[branch, u, v] for v in cols_of)))

    total[...] = (row_step(0) + row_step(1) + row_step(2)).reshape(total.shape)


def side_kernel(rows, cols, halves, branches, spots, builds):
    part, pixels = rows // halves, rows * cols

    def body(place, *refs):
        if builds:
            feat, other, taps, local_sum, halo, tall, total = refs
        else:
            tall, taps, local_sum, halo, total = refs
        lat, ch = place[0], place[1]
        width = total.shape[-1] // 2
        if builds:
            spot = pl.multiple_of((1 - lat) * (2 * pixels), pixels)
            blank = pl.multiple_of(lat * (2 * pixels), pixels)
            tall[pixels : 2 * pixels, :] = feat[...]
            tall[pl.ds(spot, pixels), :] = other[...]
            tall[pl.ds(blank, pixels), :] = jnp.zeros((pixels, tall.shape[1]), bf16)
        for index, (branch, at) in enumerate(zip(branches, spots)):
            rate = atrous_rates[branch]
            column_steps(total, tall, taps, branch, (0, 2), rows, cols)
            for half in range(halves):
                slot, its = slot_of(half, halves, ch), slice(half * part, (half + 1) * part)
                halo[slot, 1, :, at : at + rate, :] = total[its, cols - rate :, :width]
                halo[slot, 0, :, at : at + rate, :] = total[its, :rate, width:]
            local_sum[index, :, rate:, :] = total[:, : cols - rate, :width]
            local_sum[index, :, :rate, :] = jnp.zeros((rows, rate, width), f32)
            local_sum[index, :, : cols - rate, :] += total[:, rate:, width:]

    return body


def centre_kernel(rows, cols, halves):
    part = rows // halves

    def body(place, tall, taps, point_sum, *refs):
        local_sums, (out, total) = refs[: len(groups)], refs[len(groups) :]
        width = total.shape[-1]

        def store(value, lane):
            for half in range(halves):
                its = slice(half * part, (half + 1) * part)
                out[slot_of(half, halves, place[1]), :, lane * width : (lane + 1) * width] = value(
                    its
                ).reshape(part * cols, width)

        store(lambda its: point_sum[its.start * cols : its.stop * cols, :], 0)
        for number, (branches, _, _) in enumerate(groups):
            for index, branch in enumerate(branches):
                column_steps(total, tall, taps, branch, (1,), rows, cols)
                store(lambda its: total[its] + local_sums[number][index, its], branch + 1)

    return body


def head_kernel(rows, cols, width):
    pixels = rows * cols

    def body(
        place, sums, left_a, right_a, left_b, right_b,
        labels, active, scales, shifts, w_proj, proj_scale, proj_shift, w_class,
        d_point, d_side, to_left, to_right, total, grad,
    ):
        total[...] = sums[...].reshape(total.shape)
        edges = ((left_a, right_a), (left_b, right_b))
        for (branches, spots, _), (left, right) in zip(groups, edges):
            for branch, at in zip(branches, spots):
                rate = atrous_rates[branch]
                lanes = slice((branch + 1) * width, (branch + 2) * width)
                total[:, :rate, lanes] += left[:, at : at + rate, :]
                total[:, cols - rate :, lanes] += right[:, at : at + rate, :]
        scale = beside(*(scales[k : k + 1, :] for k in range(4)))
        shift = beside(*(shifts[k : k + 1, :] for k in range(4)))
        pre = total[...].reshape(pixels, 4 * width) * scale + shift
        joined = jnp.maximum(pre, 0.0).astype(bf16)
        z_pre = mul(joined, w_proj[...]) * proj_scale[...] + proj_shift[...]
        hidden = jnp.maximum(z_pre, 0.0).astype(bf16)
        logits = mul(hidden, w_class[...])
        expo = jnp.exp(logits - jnp.max(logits, axis=1, keepdims=True))
        prob = expo / jnp.sum(expo, axis=1, keepdims=True)
        ids = lax.broadcasted_iota(jnp.int32, prob.shape, 1)
        onehot = jnp.where(ids == labels[...], 1.0, 0.0)
        d_logits = (active[...] * (prob - onehot)).astype(bf16)
        d_hidden = mul_t(d_logits, w_class[...]) * proj_scale[...]
        d_z = jnp.where(z_pre > 0, d_hidden, 0.0).astype(bf16)
        d_joined = mul_t(d_z, w_proj[...]) * scale
        grad[...] = jnp.where(pre > 0, d_joined, 0.0).reshape(grad.shape)
        d_point[...] = grad[:, :, :width].astype(bf16)
        d_side[...] = grad[:, :, width:].astype(bf16)
        for branch, rate in enumerate(atrous_rates):
            at, lanes = halo_at[branch], slice((branch + 1) * width, (branch + 2) * width)
            to_left[:, at : at + rate, :] = grad[:, :rate, lanes].astype(bf16)
            to_right[:, at : at + rate, :] = grad[:, cols - rate :, lanes].astype(bf16)

    return body


def spread(
    total, field, taps, branch, steps, begin, same_band, lat, rows, part, cols
):
    rate = atrous_rates[branch]

    def add(source, target, count, u):
        weights = beside(*(taps[branch, u, v] for v in steps))
        lhs = field[pl.ds(pl.multiple_of(source * cols, cols), count * cols), :]
        product = mul_t(lhs[:, : len(steps) * weights.shape[1] // len(steps)], weights)
        total[pl.ds(target, count)] += product.reshape(count, cols, product.shape[1])

    if same_band:
        first = begin == 0
        add(0, begin, part, 1)
        inward = min(part, rows - rate)
        add(
            jnp.where(first, 0, part - inward),
            jnp.where(first, rate, rows - inward - rate),
            inward,
            jnp.where(first, 2, 0),
        )
        if part > rate:
            outward = part - rate
            add(
                jnp.where(first, rate, 0),
                jnp.where(first, 0, rows - outward),
                outward,
                jnp.where(first, 0, 2),
            )
    else:
        u = 2 * lat
        near, far = min(rate, part), rate - part
        is_near = (begin == 0) == (lat == 0) if part < rows else True

        def near_rows():
            add(lat * (part - near), (1 - lat) * (rows - rate) + lat * (rate - near), near, u)

        if part == rows:
            near_rows()
        else:
            pl.when(is_near)(near_rows)
            if far > 0:

                @pl.when(jnp.logical_not(is_near))
                def _():
                    add(lat * (part - far), (1 - lat) * (rows - rate + part), far, u)


back_order = (2, 1, 0)


def back_local_kernel(rows, cols, width, halves, mine, first):
    part = rows // halves

    def body(place, own, other, taps, *refs):
        copies = {}
        if first:
            all_taps, (total, taps, fields, arrived) = taps, refs
            copies = {
                b: pltpu.make_async_copy(all_taps.at[b], taps.at[b], arrived.at[b])
                for b in back_order
            }
            for copy in copies.values():
                copy.start()
        else:
            acc, total, fields = refs
        lat, ch = place[0], place[1]
        begin = 0 if halves == 1 else (ch if mine else 1 - ch) * part
        total[...] = jnp.zeros_like(total) if first else acc[...]
        for branch in back_order:
            rate = atrous_rates[branch]
            lanes = slice(branch * width, (branch + 1) * width)
            for source, same_band in ((own, True), (other, False)):
                field = fields.at[2 * branch + same_band]
                value = source[:, :, lanes].astype(f32)
                zeros = jnp.zeros((part, rate, width), f32)
                left = jnp.concatenate([value[:, rate:, :], zeros], 1)
                right = jnp.concatenate([zeros, value[:, : cols - rate, :]], 1)
                for step, shifted in enumerate((left, value, right)):
                    field[:, step * width : (step + 1) * width] = shifted.reshape(
                        part * cols, width
                    ).astype(bf16)
                if first and same_band:
                    copies[branch].wait()
                spread(
                    total, field, taps, branch, (0, 1, 2), begin, same_band,
                    lat, rows, part, cols,
                )

    return body


def back_halo_kernel(rows, cols, width, halves, mine, bands, last):
    part = rows // halves

    def body(place, own, other, taps, point, acc, out, fields, *refs):
        lat, ch = place[0], place[1]
        begin = 0 if halves == 1 else (ch if mine else 1 - ch) * part
        total = refs[0] if last else out
        total[...] = acc[...]
        if True in bands:
            block = own[:, 2 * halo_cols :, :].reshape(part * cols, width)
            product = mul_t(block, point[...])
            total[pl.ds(begin, part)] += product.reshape(part, cols, product.shape[1])
        for branch in back_order:
            rate, at = atrous_rates[branch], halo_at[branch]
            for same_band in bands:
                source = own if same_band else other
                field = fields.at[2 * branch + same_band]
                left = source[:, at : at + rate, :].astype(f32)
                right = source[:, halo_cols + at : halo_cols + at + rate, :].astype(f32)
                zeros = jnp.zeros((part, cols - rate, width), f32)
                for step, value in enumerate(
                    (jnp.concatenate([left, zeros], 1), jnp.concatenate([zeros, right], 1))
                ):
                    field[:, step * width : (step + 1) * width] = value.reshape(
                        part * cols, width
                    ).astype(bf16)
                spread(
                    total, field, taps, branch, (2, 0), begin, same_band,
                    lat, rows, part, cols,
                )
        if last:
            out[...] = total[...].astype(bf16)

    return body


def shift_pairs(size, step):
    return [(i, (i + step) % size) for i in range(size)]


def after(value, *first):
    return lax.optimization_barrier((value, *first))[0]


def local(
    features, labels, tile_list, w_point, w_rates, branch_scale, branch_shift,
    w_proj, proj_scale, proj_shift, w_class,
):
    rows, cols, chans = features.shape
    pixels = rows * cols
    width = w_point.shape[1]
    lon_size, ch_size, lat_size = (lax.axis_size(a) for a in ("lon", "ch", "lat"))
    assert lat_size == 2 and max(atrous_rates) <= min(rows, cols)
    halves = 2 if ch_size == 2 else 1
    part = rows // halves
    count = pixels // halves
    lat, ch = lax.axis_index("lat"), lax.axis_index("ch")
    place = jnp.stack([lat, ch]).astype(jnp.int32)
    taps = w_rates.reshape(3, 3, 3, chans, width)
    tap_flops = 2 * pixels * chans * width
    tap_bytes = 2 * chans * width

    def swap_lat(value):
        return lax.ppermute(value, "lat", shift_pairs(2, 1))

    def swap_ch(value):
        return lax.ppermute(value, "ch", shift_pairs(2, 1))

    def to_left(value):
        return lax.ppermute(value, "lon", shift_pairs(lon_size, -1))

    def to_right(value):
        return lax.ppermute(value, "lon", shift_pairs(lon_size, 1))

    gone = []

    def reduce_ch(parts):
        if halves == 2:
            sent = parts[0].astype(wire)
            gone.append(sent)
            return parts[1], swap_ch(sent)
        own = lax.psum(parts[0], "ch")
        return own, jnp.zeros(own.shape, wire)

    feat = features.reshape(pixels, chans)
    other = swap_lat(feat)
    tall_shape = shape((3 * pixels, chans), bf16)

    halos, local_sums, edges = ([None] * len(groups) for _ in range(3))

    point_sum, feat_held, taps_held = call(
        point_kernel(), "hhh",
        (
            shape((pixels, width), f32), shape((pixels, chans), bf16), shape(taps.shape, bf16),
        ),
        [pltpu.VMEM((chans, width), bf16), pltpu.SemaphoreType.DMA((3,))],
        tap_flops, 27 * tap_bytes, vmem=36,
    )(feat, w_point, taps)
    other = after(other, point_sum)

    def side_call(number, builds):
        branches, spots, group_cols = groups[number]
        shapes = [
            shape((len(branches), rows, cols, width), f32),
            shape((halves, 2, part, group_cols, width), f32),
        ]
        if builds:
            shapes.append(tall_shape)
        return call(
            side_kernel(rows, cols, halves, branches, spots, builds),
            "svvv" if builds else "svv", tuple(shapes), [pltpu.VMEM((rows, cols, 2 * width), f32)],
            6 * len(branches) * tap_flops, 6 * len(branches) * tap_bytes,
        )

    local_sums[1], halo, tall = side_call(1, True)(place, feat_held, other, taps_held)
    halos[1] = reduce_ch(halo)
    local_sums[0], halo = side_call(0, False)(place, after(tall, *gone), taps_held)
    halos[0] = reduce_ch(halo)

    def send_halo(number, *earlier):
        own, came = halos[number]
        came = after(came, *earlier)
        halo_sum = (own + came.astype(f32)).astype(wire)
        edges[number] = (to_right(halo_sum[1]), to_left(halo_sum[0]))
        return halo_sum

    sent = send_halo(1, halo)
    main = call(
        centre_kernel(rows, cols, halves), "svvv" + "v" * len(groups),
        shape((halves, count, 4 * width), f32), [pltpu.VMEM((rows, cols, width), f32)],
        10 * tap_flops, 10 * tap_bytes,
    )(place, after(tall, sent), taps_held, point_sum, *local_sums)
    own, came = reduce_ch(main)
    send_halo(0, main)

    pixel = jnp.arange(pixels, dtype=jnp.int32)
    labels, tile_list = lax.optimization_barrier((labels, tile_list, main))[:2]
    active = jnp.any(tile_list.reshape(1, -1) == (pixel // 128)[:, None], axis=1).astype(f32)
    first = ch * count if halves == 2 else 0
    label_part = lax.dynamic_slice(labels.reshape(pixels, 1), (first, 0), (count, 1))
    active_part = lax.dynamic_slice(active.reshape(pixels, 1), (first, 0), (count, 1))

    edge_shape = shape((part, halo_cols, width), bf16)
    head_field = pltpu.VMEM((part, cols, 4 * width), f32)
    operands = (
        own + came.astype(f32),
        *(e.astype(f32) for pair in edges for e in pair),
        label_part, active_part,
        branch_scale, branch_shift, w_proj,
        proj_scale.reshape(1, -1), proj_shift.reshape(1, -1), w_class,
    )
    d_point, d_side, edge_left, edge_right = call(
        head_kernel(part, cols, width), "s" + "v" * len(operands),
        (
            shape((part, cols, width), bf16), shape((part, cols, 3 * width), bf16),
            edge_shape, edge_shape,
        ),
        [head_field, head_field],
        2 * count * width * (8 * width + 2 * w_class.shape[1]), 32 * count * width,
    )(place, *operands)

    acc_shape = shape((rows, cols, chans), f32)
    out_shape = shape((rows, cols, chans), bf16)

    fields = pltpu.VMEM((6, part * cols, 3 * width), bf16)
    acc, back_taps = call(
        back_local_kernel(rows, cols, width, halves, True, True), "svvh",
        (acc_shape, shape(taps.shape, bf16)), [fields, pltpu.SemaphoreType.DMA((3,))],
        14 * tap_flops, 14 * tap_bytes, vmem=36,
    )(place, d_side, swap_lat(d_side), taps)

    def halo_taps(halo, other_halo, mine, bands, acc, last):
        return call(
            back_halo_kernel(rows, cols, width, halves, mine, bands, last),
            "svvvvv", out_shape if last else acc_shape,
            [pltpu.VMEM((6, part * cols, 2 * width), bf16)]
            + [pltpu.VMEM((rows, cols, chans), f32)] * last,
            5 * tap_flops, 14 * tap_bytes,
        )(place, halo, other_halo, back_taps, w_point, acc)

    left, right = to_right(edge_right), to_left(edge_left)
    halo_mine = jnp.concatenate([after(left, acc), right, d_point], 1)
    if halves == 2:
        d_came = after(swap_ch(d_side), acc)
        halo_came = swap_ch(halo_mine)
        both = (True, False)
        acc = halo_taps(halo_mine, swap_lat(halo_mine), True, both, acc, False)
        acc = call(
            back_local_kernel(rows, cols, width, halves, False, False), "svvvv", acc_shape,
            [fields], 14 * tap_flops, 14 * tap_bytes,
        )(place, d_came, swap_lat(d_came), back_taps, acc)
        halo_came = after(halo_came, acc)
        other_halo = swap_lat(halo_came)
        acc = halo_taps(halo_came, halo_came, False, (True,), acc, False)
        return halo_taps(halo_came, other_halo, False, (False,), acc, True)
    return halo_taps(halo_mine, swap_lat(halo_mine), True, (True, False), acc, True)


def solution(mesh):
    placed = (
        P("lat", "lon", "ch"),
        P("lat", "lon"),
        P("lat", "lon", None),
        P("ch", None),
        P(None, None, "ch", None),
        P(),
        P(),
        P(),
        P(),
        P(),
        P(),
    )
    return jax.shard_map(
        local, mesh=mesh, in_specs=placed, out_specs=P("lat", "lon", "ch"), check_vma=False
    )
```
